32 devices in a mesh: dp: 16 (over z, y, x), head: 2 (over core).
Axes of the slice: x: 2, y: 2, z: 4, core: 2. Of those that a mesh axis runs over, the one named last changes fastest.
Arguments:
- latents: bfloat16 [32768, 1280], P('dp'), may hold values from -6 to 6
- languages: int32 [128], P('dp'), may hold values from 0 to 15, never falling along the last dimension, each value on 1 to 64 neighbouring positions
- lang_table: bfloat16 [16, 1280], replicated, may hold values from -3 to 3
- norm1_gain: float32 [1280], replicated, may hold values from 0.5 to 1.5
- norm1_shift: float32 [1280], replicated, may hold values from -2 to 2
- qkv_weight: bfloat16 [1280, 3, 1280], P(None, None, 'head'), may hold values from -0.15625 to 0.15625
- out_weight: bfloat16 [1280, 1280], P('head'), may hold values from -2.5 to 2.5
- out_bias: float32 [1280], replicated, may hold values from -2 to 2
- norm2_gain: float32 [1280], replicated, may hold values from 0.5 to 1.5
- norm2_shift: float32 [1280], replicated, may hold values from -2 to 2
- up_weight: bfloat16 [1280, 1280], P(None, 'head'), may hold values from -0.15625 to 0.15625
- up_bias: float32 [1280], P('head'), may hold values from -3 to 3
- down_weight: bfloat16 [1280, 1280], P('head'), may hold values from -0.25 to 0.25
- down_bias: float32 [1280], replicated, may hold values from -2 to 2
- cotangent: bfloat16 [32768, 1280], P('dp'), may hold values from -6 to 6
Outputs:
- block_out: bfloat16 [32768, 1280], P(('dp', 'head'))
- input_grad: float32 [32768, 1280], P(('dp', 'head'))
- table_grad: float32 [16, 1280], replicated
- norm1_gain_grad: float32 [1280], replicated
- norm1_shift_grad: float32 [1280], replicated
- qkv_grad: float32 [1280, 3, 1280], P(None, None, 'head')
- out_weight_grad: float32 [1280, 1280], P('head')
- out_bias_grad: float32 [1280], replicated
- norm2_gain_grad: float32 [1280], replicated
- norm2_shift_grad: float32 [1280], replicated
- up_weight_grad: float32 [1280, 1280], P(None, 'head')
- up_bias_grad: float32 [1280], P('head')
- down_weight_grad: float32 [1280, 1280], P('head')
- down_bias_grad: float32 [1280], replicated
The draws below stay inside these ranges and needn't reach their ends.
Inputs may be any that keep to these rules, and one draw needn't show every extreme that they name: `languages`: ids never fall from one item to the next; every language has at least one item.
All inputs are finite; a program needn't handle non-finite values.
Results may differ from the reference program's by a relative error of at most 0.015.
Values may be sent and summed in bfloat16 or wider, within the bound.
No kernel may reach another device: no remote copies, remote signals or barrier semaphores. Data moves between devices by JAX's collectives and lax.ppermute only.
A program may use at most 256 MiB of HBM per device.

```python
import math
import jax
import jax.numpy as jnp
import numpy as np
from jax import lax

D = 1280
FF = 1280
HEADS = 8
LAT = 256
LANGS = 16
HEAD_DIM = 160
ITEMS = 128
TOKENS = 32768


def block_levels(stream_key, dims, shards, least, high):
    loudness, own = 1.0, jax.random.fold_in(stream_key, 6)
    for dim, parts in shards:
        draws = jnp.exp(jax.random.uniform(jax.random.fold_in(own, dim), (parts,), jnp.float32, least / len(shards), high / len(shards)))
        loudness = loudness * jnp.repeat(draws, dims[dim] // parts).reshape([-1 if axis == dim else 1 for axis in range(len(dims))])
    return loudness


def length_profile(count, total, bound, slope):
    weights = [(1 << 20) // math.isqrt(rank ** slope) + 1 for rank in range(2, count + 1)]
    spare, holding = total - bound - (count - 1), [1] * (count - 1)
    while spare > 0:
        free = [i for i in range(count - 1) if holding[i] < bound]
        mass, remaining = sum([weights[i] for i in free]), spare
        for i in free:
            extra = min(bound - holding[i], max(1, remaining * weights[i] // mass), spare)
            holding[i] = holding[i] + extra
            spare = spare - extra
    return np.array([bound] + holding)


def uneven_parts(rng, count, total, bound, lean):
    if count == 2:
        one = jax.random.randint(rng, (), max(1, total - bound), min(bound, total - 1) + 1)
        return jnp.stack([one, total - one])
    lengths = jnp.asarray(length_profile(count, total, bound, lean), jnp.int32)
    pairs = (count - 1) // 2
    giver, sink = lengths[1:1 + 2 * pairs:2], lengths[2:2 + 2 * pairs:2]
    room = jnp.minimum(giver - 1, bound - sink)
    moved = jax.random.randint(jax.random.fold_in(rng, 1), (pairs,), 0, 1 << 20) % (room + 1)
    lengths = lengths.at[1:1 + 2 * pairs:2].set(giver - moved).at[2:2 + 2 * pairs:2].set(sink + moved)
    return lengths[jax.random.permutation(jax.random.fold_in(rng, 2), count)]


def noise(own_key, extent, width, bound, shards=(), kind=jnp.bfloat16):
    array = jax.random.normal(own_key, extent, jnp.float32) * width
    if len(shards) > 0:
        array = block_levels(own_key, extent, shards, -0.22, 0.18) * array
    return jnp.clip(array, min=-bound, max=bound).astype(kind)


def setup_inputs(seed: int = 0) -> dict:
    key_of = jax.random.split(jax.random.key(seed), 16)
    return {
        "latents": noise(key_of[0], (TOKENS, D), 1.0, 6.0, ((0, 16),)),
        "languages": jnp.searchsorted(jnp.cumsum(uneven_parts(key_of[1], LANGS, ITEMS, ITEMS // 2, 2)), jnp.arange(ITEMS), side="right").astype(jnp.int32),
        "lang_table": noise(key_of[2], (LANGS, D), 0.5, 3.0),
        "norm1_gain": jnp.clip(1.0 + 0.1 * jax.random.normal(key_of[3], (D,), jnp.float32), 0.5, 1.5),
        "norm1_shift": noise(key_of[4], (D,), 0.3, 2.0, (), jnp.float32),
        "qkv_weight": noise(key_of[5], (D, 3, D), D ** -0.5, 0.15625, ((2, 2),)),
        "out_weight": noise(key_of[6], (D, D), (D // LAT) ** -0.5, 2.5, ((0, 2),)),
        "out_bias": noise(key_of[7], (D,), 0.3, 2.0, (), jnp.float32),
        "norm2_gain": jnp.clip(1.0 + 0.1 * jax.random.normal(key_of[8], (D,), jnp.float32), 0.5, 1.5),
        "norm2_shift": noise(key_of[9], (D,), 0.3, 2.0, (), jnp.float32),
        "up_weight": noise(key_of[10], (D, FF), D ** -0.5, 0.15625, ((1, 2),)),
        "up_bias": noise(key_of[11], (FF,), 0.5, 3.0, ((0, 2),), jnp.float32),
        "down_weight": noise(key_of[12], (FF, D), (FF // 2) ** -0.5, 0.25, ((0, 2),)),
        "down_bias": noise(key_of[13], (D,), 0.3, 2.0, (), jnp.float32),
        "cotangent": noise(key_of[14], (TOKENS, D), 1.0, 6.0, ((0, 16),)),
    }


EPS = 1e-05
HIGH = lax.Precision.HIGHEST

@jax.custom_vjp
def low(v):
    return lax.optimization_barrier(v.astype(jnp.bfloat16)).astype(jnp.float32)

@jax.custom_vjp
def low_back(v):
    return v

def low_keep(v):
    return (low(v), None)

def low_pass(kept, grad):
    return (grad,)

def back_keep(v):
    return (v, None)

def back_low(kept, grad):
    return (low(grad),)
low.defvjp(low_keep, low_pass)
low_back.defvjp(back_keep, back_low)

def layer_norm(v, gain, shift):
    mean = lax.optimization_barrier(jnp.mean(v, axis=-1, keepdims=True))
    centred = v - mean
    var = lax.optimization_barrier(jnp.mean(centred * centred, axis=-1, keepdims=True))
    return centred * lax.rsqrt(var + EPS) * gain + shift

def attend_item(triple):
    query, key, value = triple
    raw = jnp.einsum('qhd,khd->hqk', query, key, precision=HIGH) * HEAD_DIM ** (-0.5)
    scores = low_back(raw)
    peak = lax.optimization_barrier(jnp.max(scores, axis=-1, keepdims=True))
    weights = jnp.exp(scores - peak)
    probs = weights / lax.optimization_barrier(jnp.sum(weights, axis=-1, keepdims=True))
    return jnp.einsum('hqk,khd->qhd', low(probs), value, precision=HIGH)

def reference(latents, languages, lang_table, norm1_gain, norm1_shift, qkv_weight, out_weight, out_bias, norm2_gain, norm2_shift, up_weight, up_bias, down_weight, down_bias, cotangent):
    token_lang = jnp.repeat(languages.astype(jnp.int32), LAT)

    def forward(inputs, table, gain1, shift1, w_qkv, w_out, b_out, gain2, shift2, w_up, b_up, w_down, b_down):
        base = inputs + jnp.take(table, token_lang, axis=0)
        h_one = low(layer_norm(base, gain1, shift1))
        shaped = (ITEMS, LAT, HEADS, HEAD_DIM)
        query = low(low_back(jnp.dot(h_one, w_qkv[:, 0], precision=HIGH))).reshape(shaped)
        key = low(low_back(jnp.dot(h_one, w_qkv[:, 1], precision=HIGH))).reshape(shaped)
        value = low(low_back(jnp.dot(h_one, w_qkv[:, 2], precision=HIGH))).reshape(shaped)
        mixed = lax.map(jax.checkpoint(attend_item), (query, key, value))
        mixed = low(low_back(mixed.reshape(TOKENS, D)))
        middle = base + low_back(jnp.dot(mixed, w_out, precision=HIGH)) + b_out
        h_two = low(layer_norm(middle, gain2, shift2))
        pre = low_back(jnp.dot(h_two, w_up, precision=HIGH) + b_up)
        act = low(jax.nn.gelu(pre, approximate=True))
        return middle + jnp.dot(act, w_down, precision=HIGH) + b_down
    floats = (latents.astype(jnp.float32), lang_table.astype(jnp.float32), norm1_gain, norm1_shift, qkv_weight.astype(jnp.float32), out_weight.astype(jnp.float32), out_bias, norm2_gain, norm2_shift, up_weight.astype(jnp.float32), up_bias, down_weight.astype(jnp.float32), down_bias)
    result, backward = jax.vjp(forward, *floats)
    grads = backward(cotangent.astype(jnp.float32))
    return (result.astype(jnp.bfloat16), grads[0], grads[1], grads[2], grads[3], grads[4], grads[5], grads[6], grads[7], grads[8], grads[9], grads[10], grads[11], grads[12])
```

```python
from functools import partial

import numpy as np

import jax
import jax.numpy as jnp
from jax import lax
from jax.experimental import pallas as pl
from jax.experimental.pallas import tpu as pltpu
from jax.sharding import PartitionSpec as P

HEAD_DIM = 160
EPS = 1e-05
SCALE = HEAD_DIM ** (-0.5)
LANE = 128
WINDOW = 256
VMEM = 36 * 2**20
F32 = jnp.float32
BF16 = jnp.bfloat16
AXES = ("dp", "head")
HIGH = lax.Precision.HIGHEST
ROOT = 0.7978845608028654
CUBE = 0.044715


def dot(a, b):
    return jnp.dot(a, b, preferred_element_type=F32)


def dot_t(a, b):
    return lax.dot_general(a, b, (((1,), (1,)), ((), ())), preferred_element_type=F32)


def t_dot(a, b):
    return lax.dot_general(a, b, (((0,), (0,)), ((), ())), preferred_element_type=F32)


def row_mean(v):
    return jnp.mean(v, axis=-1, keepdims=True)


def unit_of(v):
    centred = v - row_mean(v)
    inverse = lax.rsqrt(row_mean(centred * centred) + EPS)
    return centred * inverse, inverse


def unit_back(grad, unit, inverse, gain):
    scaled = grad * gain
    return inverse * (scaled - row_mean(scaled) - unit * row_mean(scaled * unit))


def column_sum(v):
    return jnp.sum(v, axis=0, keepdims=True)


def add_to(ref, value, first):
    @pl.when(first)
    def _():
        ref[...] = value

    @pl.when(jnp.logical_not(first))
    def _():
        ref[...] += value


def table_row(tab_ref, lang):
    table = tab_ref[...].astype(F32)
    rows = lax.broadcasted_iota(jnp.int32, table.shape, 0)
    return jnp.sum(jnp.where(rows == lang, table, 0.0), axis=0, keepdims=True)


def lang_of(meta, side):
    return meta[2 + meta[side] + pl.program_id(0)]


def base_of(meta, lat_ref, tab_ref, side):
    return lat_ref[...].astype(F32) + table_row(tab_ref, lang_of(meta, side))


def head_mask(a):
    lane = lax.broadcasted_iota(jnp.int32, (1, WINDOW), 1)
    first = HEAD_DIM * a - LANE * a
    return ((lane >= first) & (lane < first + HEAD_DIM)).astype(F32).astype(BF16)


def join_heads(parts):
    lane = lax.broadcasted_iota(jnp.int32, (parts[0].shape[0], LANE), 1)
    blocks = [parts[0][:, :LANE]]
    for b in range(1, len(parts)):
        edge = HEAD_DIM * b - LANE * b
        blocks.append(jnp.where(lane < edge, parts[b - 1][:, LANE:], parts[b][:, :LANE]))
    blocks.append(parts[-1][:, LANE:])
    return jnp.concatenate(blocks, axis=1)


def windows(count):
    return [slice(LANE * a, LANE * a + WINDOW) for a in range(count)]


def attend_kernel(
    meta,
    lat_ref,
    tab_ref,
    gain_ref,
    shift_ref,
    w_ref,
    h_ref,
    proj_ref,
    prob_ref,
    mixed_ref,
    *,
    side,
):
    unit, _ = unit_of(base_of(meta, lat_ref, tab_ref, side))
    hidden = (unit * gain_ref[...] + shift_ref[...]).astype(BF16)
    h_ref[...] = hidden
    for c in range(3):
        proj_ref[c] = dot(hidden, w_ref[c]).astype(BF16)
    lanes = windows(prob_ref.shape[1])
    raw = [
        dot_t(proj_ref[0, :, w] * head_mask(a), proj_ref[1, :, w]) for a, w in enumerate(lanes)
    ]
    low = []
    for a, scores in enumerate(raw):
        scores = scores * SCALE
        weights = jnp.exp(scores - jnp.max(scores, axis=-1, keepdims=True))
        probs = weights * (1.0 / jnp.sum(weights, axis=-1, keepdims=True))
        low.append(probs.astype(BF16))
        prob_ref[0, a] = low[a]
    parts = [dot(low[a], proj_ref[2, :, w]) for a, w in enumerate(lanes)]
    mixed_ref[...] = join_heads(parts).astype(BF16)


def gelu(x):
    square = x * x
    tanh = jnp.tanh(x * (ROOT + (ROOT * CUBE) * square))
    half = 0.5 + 0.5 * tanh
    slope = half + x * (1.0 - tanh * tanh) * (0.5 * ROOT + (1.5 * ROOT * CUBE) * square)
    return x * half, slope


def feed_kernel(
    meta,
    lat_ref,
    tab_ref,
    cot_ref,
    mix0_ref,
    mix1_ref,
    out0_ref,
    out1_ref,
    down0_ref,
    down1_ref,
    up0_ref,
    up1_ref,
    upb0_ref,
    upb1_ref,
    outb_ref,
    downb_ref,
    gain_ref,
    shift_ref,
    h_ref,
    act0_ref,
    act1_ref,
    dpre0_ref,
    dpre1_ref,
    low_ref,
    dmix0_ref,
    dmix1_ref,
    block_ref,
    dgain_ref,
    dshift_ref,
    doutb_ref,
    ddownb_ref,
    dupb0_ref,
    dupb1_ref,
):
    first = pl.program_id(0) == 0
    base = base_of(meta, lat_ref, tab_ref, 0)
    attn = dot(mix0_ref[...], out0_ref[...]) + dot(mix1_ref[...], out1_ref[...])
    middle = base + attn + outb_ref[...]
    cot = cot_ref[...]
    d_act = (dot_t(cot, down0_ref[...]), dot_t(cot, down1_ref[...]))
    unit, inverse = unit_of(middle)
    hidden = (unit * gain_ref[...] + shift_ref[...]).astype(BF16)
    h_ref[...] = hidden
    pre = (dot(hidden, up0_ref[...]) + upb0_ref[...], dot(hidden, up1_ref[...]) + upb1_ref[...])
    acts, d_pres = [], []
    for j, (act_ref, dpre_ref, dupb_ref) in enumerate(
        ((act0_ref, dpre0_ref, dupb0_ref), (act1_ref, dpre1_ref, dupb1_ref))
    ):
        act, slope = gelu(pre[j])
        acts.append(act.astype(BF16))
        d_pres.append((d_act[j] * slope).astype(BF16))
        act_ref[...] = acts[j]
        dpre_ref[...] = d_pres[j]
        add_to(dupb_ref, column_sum(d_pres[j].astype(F32)), first)
    grad = dot_t(d_pres[0], up0_ref[...]) + dot_t(d_pres[1], up1_ref[...])
    out = dot(acts[0], down0_ref[...]) + dot(acts[1], down1_ref[...])
    block_ref[...] = (middle + out + downb_ref[...]).astype(BF16)
    cot = cot.astype(F32)
    d_mid = cot + unit_back(grad, unit, inverse, gain_ref[...])
    low = d_mid.astype(BF16)
    low_ref[...] = low
    dmix1_ref[...] = dot_t(low, out1_ref[...]).astype(BF16)
    dmix0_ref[...] = dot_t(low, out0_ref[...]).astype(BF16)
    add_to(dgain_ref, column_sum(grad * unit), first)
    add_to(dshift_ref, column_sum(grad), first)
    add_to(doutb_ref, column_sum(d_mid), first)
    add_to(ddownb_ref, column_sum(cot), first)


def put_pieces(piece, total, keep_ref, away_ref, table=0):
    half, rows = keep_ref.shape[-3:-1]
    groups = total.shape[0]
    for s in range(half):
        for ref, slot in ((keep_ref, s), (away_ref, s + half)):
            p = piece[2 * half * table + slot]
            start = pl.multiple_of(rows * (p // groups), 8)
            ref[s] = total[p % groups, pl.ds(start, rows), :].astype(BF16)


def attend_back_kernel(
    piece,
    h_ref,
    proj_ref,
    prob_ref,
    dmixo_ref,
    dmixp_ref,
    dproj_ref,
    *rest,
    items,
    each,
):
    outs, total = rest[:6], rest[6]
    step = pl.program_id(0)
    last = 2 * items // each - 1
    own = step < items // each
    span = proj_ref.shape[1] // each
    d_all = jnp.where(own, dmixo_ref[...], dmixp_ref[...])
    lanes = windows(prob_ref.shape[1])
    for u in range(each):
        rows = slice(span * u, span * u + span)
        d_mixed = [d_all[rows, w] for w in lanes]
        low = [prob_ref[u, a] for a in range(len(lanes))]
        d_probs = [
            dot_t(d_mixed[a] * head_mask(a), proj_ref[2, rows, w]) for a, w in enumerate(lanes)
        ]
        d_value = [t_dot(low[a], d_mixed[a]) for a in range(len(lanes))]
        d_low = []
        for a in range(len(lanes)):
            probs = low[a].astype(F32)
            d_raw = probs * (d_probs[a] - jnp.sum(probs * d_probs[a], axis=-1, keepdims=True))
            d_low.append(d_raw.astype(BF16))
        d_query = [dot(d_low[a], proj_ref[1, rows, w]) * SCALE for a, w in enumerate(lanes)]
        d_key = [t_dot(d_low[a], proj_ref[0, rows, w]) * SCALE for a, w in enumerate(lanes)]
        for c, parts in enumerate((d_query, d_key, d_value)):
            dproj_ref[c, rows] = join_heads(parts).astype(BF16)

    @pl.when(step == 0)
    def _():
        for c in range(3):
            total[c] = t_dot(h_ref[...], dproj_ref[c])

    @pl.when(step > 0)
    def _():
        for c in range(3):
            total[c] += t_dot(h_ref[...], dproj_ref[c])

    @pl.when(step == last)
    def _():
        for c in range(3):
            put_pieces(piece, total.at[c : c + 1], outs[2 * c], outs[2 * c + 1], c)


def hidden_grad_kernel(meta, dproj_ref, w_ref, out_ref):
    grad = dot_t(dproj_ref[0], w_ref[0])
    for c in range(1, 3):
        grad += dot_t(dproj_ref[c], w_ref[c])
    out_ref[...] = grad.astype(BF16)


def base_grad_kernel(
    meta,
    lat_ref,
    tab_ref,
    low_ref,
    part_ref,
    dproj_ref,
    w_ref,
    gain_ref,
    dbase_ref,
    dgain_ref,
    dshift_ref,
    dtab_ref,
):
    first = pl.program_id(0) == 0
    grad = part_ref[...].astype(F32)
    for c in range(3):
        grad += dot_t(dproj_ref[c], w_ref[c])
    unit, inverse = unit_of(base_of(meta, lat_ref, tab_ref, 0))
    d_base = low_ref[...].astype(F32) + unit_back(grad, unit, inverse, gain_ref[...])
    dbase_ref[...] = d_base
    add_to(dgain_ref, column_sum(grad * unit), first)
    add_to(dshift_ref, column_sum(grad), first)

    @pl.when(first)
    def _():
        dtab_ref[...] = jnp.zeros_like(dtab_ref)

    lang = lang_of(meta, 0)
    dtab_ref[pl.ds(lang, 1), :] += column_sum(d_base)


def weight_grad_kernel(piece, a0_ref, a1_ref, b0_ref, b1_ref, keep_ref, away_ref, total):
    step = pl.program_id(0)
    groups, _, cols = total.shape
    value = t_dot(a0_ref[...], b0_ref[...]) + t_dot(a1_ref[...], b1_ref[...])

    @pl.when(step == 0)
    def _():
        for g in range(groups):
            total[g] = value[:, cols * g : cols * g + cols]

    @pl.when(step > 0)
    def _():
        for g in range(groups):
            total[g] += value[:, cols * g : cols * g + cols]

    @pl.when(step == pl.num_programs(0) - 1)
    def _():
        put_pieces(piece, total, keep_ref, away_ref)


def plus(a, b):
    return (a.astype(F32) + b.astype(F32)).astype(BF16)


def finish_kernel(slot, near_ref, far_ref, out_ref):
    half, rows, cols = near_ref.shape
    groups = out_ref.shape[-1] // cols
    for p in range(2 * half):
        s = slot[p]
        place = lax.rem(s, half)
        value = jnp.where(
            s < half, near_ref[place].astype(F32), far_ref[place].astype(F32)
        )
        r, g = p // groups, p % groups
        out_ref[rows * r : rows * r + rows, cols * g : cols * g + cols] = value


class Line:
    def __init__(self):
        self.last = None

    def tie(self, *xs):
        if self.last is not None:
            *xs, self.last = lax.optimization_barrier((*xs, self.last))
        return xs

    def call(
        self, kernel, scalars, grid, operands, outs, scratch=(), alias=None, vmem=VMEM, mark=-1
    ):
        arrays, in_specs = zip(*operands)
        shapes, out_specs = zip(*outs)
        (scalars,) = self.tie(scalars)
        results = pl.pallas_call(
            kernel,
            out_shape=shapes,
            grid_spec=pltpu.PrefetchScalarGridSpec(
                num_scalar_prefetch=1,
                grid=grid,
                in_specs=in_specs,
                out_specs=out_specs,
                scratch_shapes=scratch,
            ),
            input_output_aliases=alias or {},
            compiler_params=pltpu.CompilerParams(vmem_limit_bytes=vmem),
            cost_estimate=pl.CostEstimate(flops=1, bytes_accessed=1, transcendentals=0),
        )(scalars, *arrays)
        if mark is not None:
            self.last = results[mark]
        return results


def shaped(shape, dtype):
    return jax.ShapeDtypeStruct(shape, dtype)


def whole(x):
    return (x, pl.BlockSpec(x.shape, lambda i, meta: (0,) * x.ndim, pipeline_mode=pl.Buffered(1)))


def whole_out(shape, dtype):
    return (shaped(shape, dtype), pl.BlockSpec(shape, lambda i, meta: (0,) * len(shape)))


def any_place(x):
    return (x, pl.BlockSpec(memory_space=pl.ANY))


def row_blocks(x, span, first=0):
    lead = x.shape[:-2]
    spec = pl.BlockSpec(
        lead + (span, x.shape[-1]), lambda i, meta: (0,) * len(lead) + (first + i, 0)
    )
    return (x, spec)


def local_blocks(x, span, side):
    return (x, pl.BlockSpec((span, x.shape[-1]), lambda i, meta: (meta[side] + i, 0)))


def item_blocks(x, each=1, first=0):
    lead = (0,) * (x.ndim - 1)
    return (x, pl.BlockSpec((each,) + x.shape[1:], lambda i, meta: (first + i,) + lead))


def swap(x):
    return lax.ppermute(x, "head", [(0, 1), (1, 0)])


class Sums:
    def __init__(self, line, n_dp, n_head):
        self.line, self.n_dp, self.n_head = line, n_dp, n_head
        self.bits = n_dp.bit_length() - 1
        self.me = lax.axis_index("dp")
        self.head = lax.axis_index("head")
        self.tables = {}

    def order(self, *first):
        bits = [b for b in first if b < self.bits]
        bits += [b for b in range(self.bits) if b not in bits]
        swapped = [{0: 1, 1: 0}.get(b, b) if self.bits > 1 else b for b in bits]
        return (tuple(bits), tuple(swapped))

    def table(self, order):
        if order not in self.tables:
            slots = np.arange(self.n_dp)
            to_piece = np.zeros((self.n_head, self.n_dp), np.int32)
            for h in range(self.n_head):
                for s, bit in enumerate(order[h]):
                    to_piece[h] |= ((slots >> (self.bits - 1 - s)) & 1) << bit
            to_slot = np.argsort(to_piece, axis=1).astype(np.int32)
            here = jnp.arange(self.n_dp, dtype=jnp.int32) ^ self.me
            piece_of = jnp.where(self.head == 0, to_piece[0], to_piece[1]) ^ self.me
            slot_of = jnp.where(
                self.head == 0, jnp.asarray(to_slot[0])[here], jnp.asarray(to_slot[1])[here]
            )
            self.tables[order] = (piece_of.astype(jnp.int32), slot_of.astype(jnp.int32))
        return self.tables[order]

    def send(self, x, order, stage):
        perm = []
        for d in range(self.n_dp):
            for h in range(self.n_head):
                to = d ^ (1 << order[h][stage])
                perm.append((d * self.n_head + h, to * self.n_head + h))
        return lax.ppermute(x, AXES, perm)

    def piece_shape(self, m, n):
        return (m * n // (self.n_dp * 640), 640)

    def halves_out(self, m, n):
        return [whole_out((self.n_dp // 2,) + self.piece_shape(m, n), BF16)] * 2

    def weight_grad(self, a0, a1, b0, b1, step, order):
        rows, m = a0[0].shape
        n = b0[0].shape[-1]
        groups = n // 640
        return self.line.call(
            weight_grad_kernel,
            jnp.concatenate([self.table(order)[0], self.meta]),
            (rows // step,),
            [a0, a1, b0, b1],
            self.halves_out(m, n),
            [pltpu.VMEM((groups, m, 640), F32)],
        )

    def reduce(self, keep, away, order, finish):
        for stage in range(self.bits):
            got = self.send(away, order, stage)
            yield
            keep, got = self.line.tie(keep, got)
            half = keep.shape[0] // 2
            if half:
                keep, away = plus(keep[:half], got[:half]), plus(keep[half:], got[half:])
                self.line.last = away
            else:
                keep = plus(keep, got)
                self.line.last = keep
        for stage in reversed(range(1, self.bits)):
            got = self.send(keep, order, stage)
            yield
            keep, got = self.line.tie(keep, got)
            keep = jnp.concatenate([keep, got], axis=0)
            self.line.last = keep
        got = self.send(keep, order, 0)
        yield
        finish(keep, got)
        yield

    def finish(self, near, far, order, shape):
        (result,) = self.line.call(
            finish_kernel,
            self.table(order)[1],
            (1,),
            [whole(near), whole(far)],
            [whole_out(shape, F32)],
        )
        return result

    def finish3(self, parts, orders, shape):
        scalars = jnp.concatenate([self.table(order)[1] for order in orders])
        operands = [whole(x) for pair in parts for x in pair]

        def kernel(slot, *refs):
            out_ref = refs[-1]
            for c in range(3):

                @pl.when(pl.program_id(0) == c)
                def _(c=c):
                    finish_kernel(
                        slot.at[pl.ds(self.n_dp * c, self.n_dp)],
                        refs[2 * c],
                        refs[2 * c + 1],
                        out_ref.at[0],
                    )

        spec = pl.BlockSpec((1,) + shape[1:], lambda i, slot: (i, 0, 0))
        (result,) = self.line.call(
            kernel, scalars, (3,), operands, [(shaped(shape, F32), spec)], vmem=40 * 2**20
        )
        return result


def sum_small(line, x, total, finish):
    bit = 1
    while bit < total:
        got = lax.ppermute(x, AXES, [(i, i ^ bit) for i in range(total)])
        yield
        x, got = line.tie(x, got)
        x = x + got
        line.last = x
        bit *= 2
    finish(x)
    yield


def body(
    latents,
    languages,
    lang_table,
    norm1_gain,
    norm1_shift,
    qkv_weight,
    out_weight,
    out_bias,
    norm2_gain,
    norm2_shift,
    up_weight,
    up_bias,
    down_weight,
    down_bias,
    cotangent,
):
    n_dp, n_head = lax.axis_size("dp"), lax.axis_size("head")
    head = lax.axis_index("head")
    width = latents.shape[1]
    half = width // 2
    heads = half // HEAD_DIM
    span = latents.shape[0] // languages.shape[0]
    rows = latents.shape[0] // 2
    items = rows // span
    starts = jnp.stack([head * items, (1 - head) * items]).astype(jnp.int32)
    meta = jnp.concatenate([starts, languages.astype(jnp.int32)])
    line = Line()
    call = line.call
    sums = Sums(line, n_dp, n_head)
    sums.meta = starts
    plane = sums.order(0, 1, 2, 3)
    tall = sums.order(2, 0, 1, 3)
    qkv_orders = (plane, plane, tall)

    def one_row(v):
        return v.reshape(1, -1)

    qkv = jnp.transpose(qkv_weight, (1, 0, 2))
    wo = (out_weight, swap(out_weight))
    wu = (up_weight, swap(up_weight))
    wd = (down_weight, swap(down_weight))
    ub = (one_row(up_bias), one_row(swap(up_bias)))

    lat = local_blocks(latents, span, 0)
    cot = local_blocks(cotangent, span, 0)
    tab = whole(lang_table)
    gain1, shift1 = whole(one_row(norm1_gain)), whole(one_row(norm1_shift))
    gain2, shift2 = whole(one_row(norm2_gain)), whole(one_row(norm2_shift))

    def rows_out(cols, dtype, lead=()):
        shape = shaped(lead + (rows, cols), dtype)
        return (shape, row_blocks(shape, span)[1])

    def sum_out(*shape):
        return whole_out(shape, F32)

    def half_out(shape, spec):
        return (shape, spec)

    grid = (items,)
    h1_shape = shaped((2 * rows, width), BF16)
    proj_shape = shaped((3, 2 * rows, half), BF16)
    prob_shape = shaped((2 * items, heads, span, span), BF16)

    def attend_side(side, into):
        first = side * items
        operands = [local_blocks(latents, span, side), tab, gain1, shift1, whole(qkv)]
        alias = None
        if into is not None:
            operands += [any_place(x) for x in into]
            alias = {1 + 5 + i: i for i in range(3)}

        def kernel(meta, *refs):
            attend_kernel(meta, *refs[:5], *refs[len(operands) :], side=side)

        return call(
            kernel,
            meta,
            grid,
            operands,
            [
                row_blocks(h1_shape, span, first),
                row_blocks(proj_shape, span, first),
                item_blocks(prob_shape, 1, first),
                rows_out(half, BF16),
            ],
            alias=alias,
        )

    h1, proj, prob, mixed_p = attend_side(1, None)
    mixed_x = swap(mixed_p)
    h1, proj, prob, mixed_o = attend_side(0, (h1, proj, prob))
    h2, act0, act1, dpre0, dpre1, low, dmix0, dmix1, block_out, *sums2 = call(
        feed_kernel,
        meta,
        grid,
        [lat, tab, cot, row_blocks(mixed_o, span), row_blocks(mixed_x, span)]
        + [whole(wo[0]), whole(wo[1]), whole(wd[0]), whole(wd[1]), whole(wu[0]), whole(wu[1])]
        + [whole(ub[0]), whole(ub[1]), whole(one_row(out_bias)), whole(one_row(down_bias))]
        + [gain2, shift2],
        [rows_out(width, BF16)]
        + [rows_out(half, BF16)] * 4
        + [rows_out(width, BF16), rows_out(half, BF16), rows_out(half, BF16)]
        + [rows_out(width, BF16)]
        + [sum_out(1, width)] * 4
        + [sum_out(1, half)] * 2,
        vmem=58 * 2**20,
        mark=0,
    )
    dgain2, dshift2, dbias, ddownb, dupb0, dupb1 = sums2
    act_x = swap(act1)
    dpre_x = swap(dpre1)
    h2_x = swap(h2)
    low_x = swap(low)
    dmix_x = swap(dmix1)

    step = min(rows, 512)
    steps = rows // step

    def shared(x, side):
        return (
            x,
            pl.BlockSpec(
                (step, x.shape[-1]), lambda i, s: (s[n_dp + side] * span // step + i, 0)
            ),
        )

    def blocks(x):
        return row_blocks(x, step)

    results = {}

    def keep_result(name, shape, order):
        def finish(near, far):
            results[name] = sums.finish(near, far, order, shape)

        return finish

    def keep_parts(c):
        def finish(near, far):
            results[c] = (near, far)

        return finish

    def advance(*chains):
        for chain in chains:
            next(chain)

    keep, away = sums.weight_grad(
        blocks(act0), blocks(act_x), shared(cotangent, 0), shared(cotangent, 1), step, plane
    )
    down = sums.reduce(keep, away, plane, keep_result("down", down_weight.shape, plane))
    advance(down)
    keep, away = sums.weight_grad(
        blocks(h2), blocks(h2_x), blocks(dpre0), blocks(dpre_x), step, plane
    )
    up = sums.reduce(keep, away, plane, keep_result("up", up_weight.shape, plane))
    advance(up, down)
    keep, away = sums.weight_grad(
        blocks(mixed_o), blocks(mixed_p), blocks(low), blocks(low_x), step, plane
    )
    out = sums.reduce(keep, away, plane, keep_result("out", out_weight.shape, plane))
    advance(out, up, down)

    each = 2 if items % 2 == 0 else 1
    count = items // each
    wide = each * span
    qkv_halves = sums.halves_out(width, half)
    dproj_shape = shaped((3, 2 * rows, half), BF16)
    dmix_own = pl.BlockSpec((wide, half), lambda i, s: (jnp.minimum(i, count - 1), 0))
    dmix_other = pl.BlockSpec((wide, half), lambda i, s: (jnp.maximum(i - count, 0), 0))
    dproj, *pieces = call(
        partial(attend_back_kernel, items=items, each=each),
        jnp.concatenate([sums.table(order)[0] for order in qkv_orders]),
        (2 * count,),
        [row_blocks(h1, wide), row_blocks(proj, wide), item_blocks(prob, each)]
        + [(dmix0, dmix_own), (dmix_x, dmix_other)],
        [row_blocks(dproj_shape, wide)] + qkv_halves * 3,
        [pltpu.VMEM((3, width, half), F32)],
        vmem=50 * 2**20,
        mark=0,
    )
    qkv_chains = [
        sums.reduce(pieces[2 * c], pieces[2 * c + 1], qkv_orders[c], keep_parts(c))
        for c in range(3)
    ]
    advance(*qkv_chains)
    advance(out, up, down)
    (part,) = call(
        hidden_grad_kernel,
        meta,
        grid,
        [row_blocks(dproj, span, items), whole(qkv)],
        [rows_out(width, BF16)],
    )
    advance(out, up, down)
    (part,) = line.tie(part)
    part_x = swap(part)
    advance(*qkv_chains)
    advance(out, up, down)
    dbase, dgain1, dshift1, dtab = call(
        base_grad_kernel,
        meta,
        grid,
        [lat, tab, row_blocks(low, span), row_blocks(part_x, span)]
        + [row_blocks(dproj, span), whole(qkv), gain1],
        [rows_out(width, F32), sum_out(1, width), sum_out(1, width)]
        + [sum_out(*lang_table.shape)],
    )
    dupb = jnp.where(
        head == 0,
        jnp.concatenate([dupb0, dupb1], axis=1),
        jnp.concatenate([dupb1, dupb0], axis=1),
    )
    small = jnp.concatenate([dtab, dgain1, dshift1, dbias, dgain2, dshift2, ddownb, dupb], axis=0)
    small = sum_small(line, small, n_dp * n_head, lambda x: results.update(small=x))
    chains = qkv_chains + [out, up, down, small]
    live = list(chains)
    while live:
        for chain in list(live):
            if next(chain, "end") == "end":
                live.remove(chain)
    dqkv = sums.finish3([results[c] for c in range(3)], qkv_orders, qkv.shape)
    small = results["small"]
    langs = lang_table.shape[0]
    dgain1, dshift1, dbias, dgain2, dshift2, ddownb, dupb = [small[langs + i] for i in range(7)]
    dupb = lax.dynamic_slice_in_dim(dupb, head * half, half, 0)
    return (
        block_out,
        dbase,
        small[:langs],
        dgain1,
        dshift1,
        jnp.transpose(dqkv, (1, 0, 2)),
        results["out"],
        dbias,
        dgain2,
        dshift2,
        results["up"],
        dupb,
        results["down"],
        ddownb,
    )


def normalize(values, gain, shift):
    mean = jnp.mean(values, axis=-1, keepdims=True)
    centred = values - mean
    inverse = lax.rsqrt(jnp.mean(centred * centred, axis=-1, keepdims=True) + EPS)
    unit = centred * inverse
    return (unit * gain + shift, unit, inverse)


def normalize_back(grad, unit, inverse, gain):
    scaled = grad * gain
    return inverse * (
        scaled
        - jnp.mean(scaled, axis=-1, keepdims=True)
        - unit * jnp.mean(scaled * unit, axis=-1, keepdims=True)
    )


def own_rows(values, start, share):
    return lax.dynamic_slice_in_dim(values, start, share, 0)


def plain_body(
    latents,
    languages,
    lang_table,
    norm1_gain,
    norm1_shift,
    qkv_weight,
    out_weight,
    out_bias,
    norm2_gain,
    norm2_shift,
    up_weight,
    up_bias,
    down_weight,
    down_bias,
    cotangent,
):
    f32 = jnp.float32
    bf16 = jnp.bfloat16
    items = languages.shape[0]
    rows = latents.shape[0]
    span = rows // items
    width = latents.shape[1]
    local = qkv_weight.shape[2]
    heads_here = local // HEAD_DIM
    scale = HEAD_DIM ** (-0.5)
    share = rows // lax.axis_size("head")
    start = lax.axis_index("head") * share
    token_lang = jnp.repeat(languages, span)
    onehot = (
        token_lang[:, None] == jnp.arange(lang_table.shape[0], dtype=jnp.int32)[None, :]
    ).astype(bf16)
    base = latents.astype(f32) + jnp.dot(onehot, lang_table, preferred_element_type=f32)
    normed1, unit1, inverse1 = normalize(base, norm1_gain, norm1_shift)
    h_one = normed1.astype(bf16)
    qkv_flat = qkv_weight.reshape(width, 3 * local)
    proj = jnp.dot(h_one, qkv_flat, preferred_element_type=f32).astype(bf16)
    proj = proj.reshape(items, span, 3, heads_here, HEAD_DIM)
    query = proj[:, :, 0]
    key = proj[:, :, 1]
    value = proj[:, :, 2]
    raw = jnp.einsum("iqhd,ikhd->ihqk", query, key, preferred_element_type=f32) * scale
    peak = jnp.max(raw, axis=-1, keepdims=True)
    weights = jnp.exp(raw - peak)
    probs = weights / jnp.sum(weights, axis=-1, keepdims=True)
    probs_low = probs.astype(bf16)
    mixed = jnp.einsum("ihqk,ikhd->iqhd", probs_low, value, preferred_element_type=f32)
    mixed = mixed.astype(bf16).reshape(rows, local)
    attn_part = jnp.dot(mixed, out_weight, preferred_element_type=f32)
    attn_full = lax.psum(attn_part, "head")
    middle = base + attn_full + out_bias
    normed2, unit2, inverse2 = normalize(middle, norm2_gain, norm2_shift)
    h_two = normed2.astype(bf16)
    pre = jnp.dot(h_two, up_weight, preferred_element_type=f32) + up_bias
    act, gelu_back = jax.vjp(partial(jax.nn.gelu, approximate=True), pre)
    act_low = act.astype(bf16)
    down_part = jnp.dot(act_low, down_weight, preferred_element_type=f32)
    final = (
        middle + lax.psum(down_part.astype(jnp.bfloat16), "head").astype(jnp.float32) + down_bias
    )
    block_out = own_rows(final, start, share).astype(bf16)
    grad_rows = cotangent.astype(f32)
    d_act = jnp.einsum("td,fd->tf", cotangent, down_weight, preferred_element_type=f32)
    d_down = jnp.einsum("tf,td->fd", act_low, cotangent, preferred_element_type=f32)
    d_pre_low = gelu_back(d_act)[0].astype(bf16)
    d_up = jnp.einsum("td,tf->df", h_two, d_pre_low, preferred_element_type=f32)
    d_up_bias = jnp.sum(d_pre_low.astype(f32), axis=0)
    h2_part = jnp.einsum("tf,df->td", d_pre_low, up_weight, preferred_element_type=f32)
    h2_grad = lax.psum(h2_part, "head")
    d_middle = grad_rows + normalize_back(h2_grad, unit2, inverse2, norm2_gain)
    d_middle_low = d_middle.astype(bf16)
    d_gain2 = jnp.sum(h2_grad * unit2, axis=0)
    d_shift2 = jnp.sum(h2_grad, axis=0)
    d_out_bias = jnp.sum(d_middle, axis=0)
    d_down_bias = jnp.sum(grad_rows, axis=0)
    d_out = jnp.einsum("tc,td->cd", mixed, d_middle_low, preferred_element_type=f32)
    d_mixed = jnp.einsum("td,cd->tc", d_middle_low, out_weight, preferred_element_type=f32)
    d_mixed = d_mixed.astype(bf16).reshape(items, span, heads_here, HEAD_DIM)
    d_probs = jnp.einsum("iqhd,ikhd->ihqk", d_mixed, value, preferred_element_type=f32)
    d_value = jnp.einsum("ihqk,iqhd->ikhd", probs_low, d_mixed, preferred_element_type=f32)
    d_raw = probs * (d_probs - jnp.sum(probs * d_probs, axis=-1, keepdims=True))
    d_raw_low = d_raw.astype(bf16)
    d_query = jnp.einsum("ihqk,ikhd->iqhd", d_raw_low, key, preferred_element_type=f32) * scale
    d_key = jnp.einsum("ihqk,iqhd->ikhd", d_raw_low, query, preferred_element_type=f32) * scale
    d_proj = jnp.stack([d_query, d_key, d_value], axis=2).astype(bf16).reshape(rows, 3 * local)
    d_qkv = jnp.einsum("td,tc->dc", h_one, d_proj, preferred_element_type=f32).reshape(
        width, 3, local
    )
    h1_part = jnp.einsum("tc,dc->td", d_proj, qkv_flat, preferred_element_type=f32)
    h1_grad = lax.psum(h1_part.astype(jnp.bfloat16), "head").astype(jnp.float32)
    d_base = d_middle + normalize_back(h1_grad, unit1, inverse1, norm1_gain)
    onehot_own = onehot.astype(f32)
    input_grad = own_rows(d_base, start, share)
    d_gain1 = jnp.sum(h1_grad * unit1, axis=0)
    d_shift1 = jnp.sum(h1_grad, axis=0)
    d_table = jnp.einsum("tl,td->ld", onehot_own, d_base, precision=HIGH)
    (
        d_qkv,
        d_out,
        d_up,
        d_up_bias,
        d_down,
        d_table,
        d_gain1,
        d_shift1,
        d_out_bias,
        d_gain2,
        d_shift2,
        d_down_bias,
    ) = (
        lax.psum(d_qkv.astype(jnp.bfloat16), "dp").astype(jnp.float32),
        lax.psum(d_out.astype(jnp.bfloat16), "dp").astype(jnp.float32),
        lax.psum(d_up.astype(jnp.bfloat16), "dp").astype(jnp.float32),
        lax.psum(d_up_bias.astype(jnp.bfloat16), "dp").astype(jnp.float32),
        lax.psum(d_down.astype(jnp.bfloat16), "dp").astype(jnp.float32),
        lax.psum(d_table.astype(jnp.bfloat16), "dp").astype(jnp.float32),
        lax.psum(d_gain1.astype(jnp.bfloat16), "dp").astype(jnp.float32),
        lax.psum(d_shift1.astype(jnp.bfloat16), "dp").astype(jnp.float32),
        lax.psum(d_out_bias.astype(jnp.bfloat16), "dp").astype(jnp.float32),
        lax.psum(d_gain2.astype(jnp.bfloat16), "dp").astype(jnp.float32),
        lax.psum(d_shift2.astype(jnp.bfloat16), "dp").astype(jnp.float32),
        lax.psum(d_down_bias.astype(jnp.bfloat16), "dp").astype(jnp.float32),
    )
    return (
        block_out,
        input_grad,
        d_table,
        d_gain1,
        d_shift1,
        d_qkv,
        d_out,
        d_out_bias,
        d_gain2,
        d_shift2,
        d_up,
        d_up_bias,
        d_down,
        d_down_bias,
    )


def solution(mesh):
    in_specs = (
        P("dp", None),
        P("dp"),
        P(),
        P(),
        P(),
        P(None, None, "head"),
        P("head", None),
        P(),
        P(),
        P(),
        P(None, "head"),
        P("head"),
        P("head", None),
        P(),
        P("dp", None),
    )
    out_specs = (
        P(("dp", "head"), None),
        P(("dp", "head"), None),
        P(),
        P(),
        P(),
        P(None, None, "head"),
        P("head", None),
        P(),
        P(),
        P(),
        P(None, "head"),
        P("head"),
        P("head", None),
        P(),
    )
    return jax.shard_map(
        body if mesh.shape["head"] == 2 else plain_body,
         mesh=mesh, in_specs=in_specs, out_specs=out_specs, check_vma=False)
```

```python
from functools import partial

import numpy as np

import jax
import jax.numpy as jnp
from jax import lax
from jax.experimental import pallas as pl
from jax.experimental.pallas import tpu as pltpu
from jax.sharding import PartitionSpec as P

HEAD_DIM = 160
EPS = 1e-05
SCALE = HEAD_DIM ** (-0.5)
LANE = 128
WINDOW = 256
VMEM = 60 * 2**20
F32 = jnp.float32
BF16 = jnp.bfloat16
AXES = ("dp", "head")
HIGH = lax.Precision.HIGHEST
ROOT = 0.7978845608028654
CUBE = 0.044715


def dot(a, b):
    return jnp.dot(a, b, preferred_element_type=F32)


def dot_t(a, b):
    return lax.dot_general(a, b, (((1,), (1,)), ((), ())), preferred_element_type=F32)


def t_dot(a, b):
    return lax.dot_general(a, b, (((0,), (0,)), ((), ())), preferred_element_type=F32)


def row_mean(v):
    return jnp.mean(v, axis=-1, keepdims=True)


def unit_of(v):
    centred = v - row_mean(v)
    inverse = lax.rsqrt(row_mean(centred * centred) + EPS)
    return centred * inverse, inverse


def unit_back(grad, unit, inverse, gain):
    scaled = grad * gain
    return inverse * (scaled - row_mean(scaled) - unit * row_mean(scaled * unit))


def column_sum(v):
    return jnp.sum(v, axis=0, keepdims=True)


def line_of(ref):
    return ref[...].reshape(1, -1)


def add_to(ref, value, first):
    @pl.when(first)
    def _():
        ref[...] = value

    @pl.when(jnp.logical_not(first))
    def _():
        ref[...] += value


def table_row(tab_ref, lang):
    table = tab_ref[...].astype(F32)
    rows = lax.broadcasted_iota(jnp.int32, table.shape, 0)
    return jnp.sum(jnp.where(rows == lang, table, 0.0), axis=0, keepdims=True)


def lang_of(meta, side, at):
    return meta[at + meta[side] + pl.program_id(0)]


def base_of(meta, lat_ref, tab_ref, side, at):
    return lat_ref[...].astype(F32) + table_row(tab_ref, lang_of(meta, side, at))


def head_mask(a):
    lane = lax.broadcasted_iota(jnp.int32, (1, WINDOW), 1)
    first = HEAD_DIM * a - LANE * a
    return ((lane >= first) & (lane < first + HEAD_DIM)).astype(F32).astype(BF16)


def join_heads(parts):
    lane = lax.broadcasted_iota(jnp.int32, (parts[0].shape[0], LANE), 1)
    blocks = [parts[0][:, :LANE]]
    for b in range(1, len(parts)):
        edge = HEAD_DIM * b - LANE * b
        blocks.append(jnp.where(lane < edge, parts[b - 1][:, LANE:], parts[b][:, :LANE]))
    blocks.append(parts[-1][:, LANE:])
    return jnp.concatenate(blocks, axis=1)


def windows(count):
    return [slice(LANE * a, LANE * a + WINDOW) for a in range(count)]


STEPS = ("T1", "WD", "T2", 0, "WU", 1, "WO", 2, "B", 1, "H1", 2, "T3", 4, "H2", 33, "F", "F", "F")
SENDS = (0, 1, 2)
CROSS = {"down": (0, 1, 2, 3), "up": (0, 2, 1, 3), "out": (2, 0, 1, 3), 0: (0, 1, 2, 3), 1: (0, 2, 1, 3), 2: (2, 0, 1, 3)}


def attend_kernel(
    meta,
    lat_ref,
    tab_ref,
    gain_ref,
    shift_ref,
    w_ref,
    h_ref,
    proj_ref,
    prob_ref,
    mixed_ref,
    *,
    side,
    at,
):
    unit, _ = unit_of(base_of(meta, lat_ref, tab_ref, side, at))
    hidden = (unit * line_of(gain_ref) + line_of(shift_ref)).astype(BF16)
    h_ref[...] = hidden
    for c in range(3):
        proj_ref[c] = dot(hidden, w_ref[c]).astype(BF16)
    lanes = windows(prob_ref.shape[1])
    raw = [
        dot_t(proj_ref[0, :, w] * head_mask(a), proj_ref[1, :, w]) for a, w in enumerate(lanes)
    ]
    low = []
    for a, scores in enumerate(raw):
        scores = scores * SCALE
        weights = jnp.exp(scores - jnp.max(scores, axis=-1, keepdims=True))
        probs = weights * (1.0 / jnp.sum(weights, axis=-1, keepdims=True))
        low.append(probs.astype(BF16))
        prob_ref[0, a] = low[a]
    parts = [dot(low[a], proj_ref[2, :, w]) for a, w in enumerate(lanes)]
    mixed_ref[...] = join_heads(parts).astype(BF16)


def gelu(x):
    square = x * x
    tanh = jnp.tanh(x * (ROOT + (ROOT * CUBE) * square))
    half = 0.5 + 0.5 * tanh
    slope = half + x * (1.0 - tanh * tanh) * (0.5 * ROOT + (1.5 * ROOT * CUBE) * square)
    return x * half, slope


def feed_kernel(
    meta,
    lat_ref,
    tab_ref,
    cot_ref,
    mix0_ref,
    mix1_ref,
    out0_ref,
    out1_ref,
    down0_ref,
    down1_ref,
    up0_ref,
    up1_ref,
    upb0_ref,
    upb1_ref,
    outb_ref,
    downb_ref,
    gain_ref,
    shift_ref,
    h_ref,
    act0_ref,
    act1_ref,
    dpre0_ref,
    dpre1_ref,
    low_ref,
    dmix0_ref,
    dmix1_ref,
    block_ref,
    dgain_ref,
    dshift_ref,
    doutb_ref,
    ddownb_ref,
    dupb0_ref,
    dupb1_ref,
    *,
    at,
):
    first = pl.program_id(0) == 0
    base = base_of(meta, lat_ref, tab_ref, 0, at)
    attn = dot(mix0_ref[...], out0_ref[...]) + dot(mix1_ref[...], out1_ref[...])
    middle = base + attn + line_of(outb_ref)
    cot = cot_ref[...]
    d_act = (dot_t(cot, down0_ref[...]), dot_t(cot, down1_ref[...]))
    unit, inverse = unit_of(middle)
    hidden = (unit * line_of(gain_ref) + line_of(shift_ref)).astype(BF16)
    h_ref[...] = hidden
    pre = (dot(hidden, up0_ref[...]) + line_of(upb0_ref), dot(hidden, up1_ref[...]) + line_of(upb1_ref))
    acts, d_pres = [], []
    for j, (act_ref, dpre_ref, dupb_ref) in enumerate(
        ((act0_ref, dpre0_ref, dupb0_ref), (act1_ref, dpre1_ref, dupb1_ref))
    ):
        act, slope = gelu(pre[j])
        acts.append(act.astype(BF16))
        d_pres.append((d_act[j] * slope).astype(BF16))
        act_ref[...] = acts[j]
        dpre_ref[...] = d_pres[j]
        add_to(dupb_ref, column_sum(d_pres[j].astype(F32)), first)
    grad = dot_t(d_pres[0], up0_ref[...]) + dot_t(d_pres[1], up1_ref[...])
    out = dot(acts[0], down0_ref[...]) + dot(acts[1], down1_ref[...])
    block_ref[...] = (middle + out + line_of(downb_ref)).astype(BF16)
    cot = cot.astype(F32)
    d_mid = cot + unit_back(grad, unit, inverse, line_of(gain_ref))
    low = d_mid.astype(BF16)
    low_ref[...] = low
    dmix1_ref[...] = dot_t(low, out1_ref[...]).astype(BF16)
    dmix0_ref[...] = dot_t(low, out0_ref[...]).astype(BF16)
    add_to(dgain_ref, column_sum(grad * unit), first)
    add_to(dshift_ref, column_sum(grad), first)
    add_to(doutb_ref, column_sum(d_mid), first)
    add_to(ddownb_ref, column_sum(cot), first)


def put_pieces(table, at, total, keep_ref, away_ref):
    half, rows = keep_ref.shape[-3:-1]
    groups = total.shape[0]
    for s in range(half):
        for ref, slot in ((keep_ref, s), (away_ref, s + half)):
            p = table[at + slot]
            start = pl.multiple_of(rows * (p // groups), 8)
            ref[s] = total[p % groups, pl.ds(start, rows), :].astype(BF16)


def attend_back_kernel(
    table,
    h_ref,
    proj_ref,
    prob_ref,
    dmixo_ref,
    dmixp_ref,
    dproj_ref,
    *rest,
    items,
    each,
    at,
):
    outs, total = rest[:6], rest[6]
    step = pl.program_id(0)
    last = 2 * items // each - 1
    own = step < items // each
    span = proj_ref.shape[1] // each
    d_all = jnp.where(own, dmixo_ref[...], dmixp_ref[...])
    lanes = windows(prob_ref.shape[1])
    for u in range(each):
        rows = slice(span * u, span * u + span)
        d_mixed = [d_all[rows, w] for w in lanes]
        low = [prob_ref[u, a] for a in range(len(lanes))]
        d_probs = [
            dot_t(d_mixed[a] * head_mask(a), proj_ref[2, rows, w]) for a, w in enumerate(lanes)
        ]
        d_value = [t_dot(low[a], d_mixed[a]) for a in range(len(lanes))]
        d_low = []
        for a in range(len(lanes)):
            probs = low[a].astype(F32)
            d_raw = probs * (d_probs[a] - jnp.sum(probs * d_probs[a], axis=-1, keepdims=True))
            d_low.append(d_raw.astype(BF16))
        d_query = [dot(d_low[a], proj_ref[1, rows, w]) * SCALE for a, w in enumerate(lanes)]
        d_key = [t_dot(d_low[a], proj_ref[0, rows, w]) * SCALE for a, w in enumerate(lanes)]
        for c, parts in enumerate((d_query, d_key, d_value)):
            dproj_ref[c, rows] = join_heads(parts).astype(BF16)

    @pl.when(step == 0)
    def _():
        for c in range(3):
            total[c] = t_dot(h_ref[...], dproj_ref[c])

    @pl.when(step > 0)
    def _():
        for c in range(3):
            total[c] += t_dot(h_ref[...], dproj_ref[c])

    @pl.when(step == last)
    def _():
        for c in range(3):
            put_pieces(table, at[c], total.at[c : c + 1], outs[2 * c], outs[2 * c + 1])


def hidden_grad_kernel(meta, dproj_ref, w_ref, *out_refs):
    grad = dot_t(dproj_ref[0], w_ref[0])
    for c in range(1, 3):
        grad += dot_t(dproj_ref[c], w_ref[c])
    for i, out_ref in enumerate(out_refs):

        @pl.when(pl.program_id(0) == i)
        def _(out_ref=out_ref):
            out_ref[...] = grad.astype(BF16)


def base_grad_kernel(meta, *refs, at):
    part_refs = refs[:-10]
    lat_ref, tab_ref, low_ref, dproj_ref, w_ref, gain_ref = refs[-10:-4]
    dbase_ref, dgain_ref, dshift_ref, dtab_ref = refs[-4:]
    first = pl.program_id(0) == 0
    part = part_refs[0][...]
    for i in range(1, len(part_refs)):
        part = jnp.where(pl.program_id(0) == i, part_refs[i][...], part)
    grad = part.astype(F32)
    for c in range(3):
        grad += dot_t(dproj_ref[c], w_ref[c])
    unit, inverse = unit_of(base_of(meta, lat_ref, tab_ref, 0, at))
    d_base = low_ref[...].astype(F32) + unit_back(grad, unit, inverse, line_of(gain_ref))
    dbase_ref[...] = d_base
    add_to(dgain_ref, column_sum(grad * unit), first)
    add_to(dshift_ref, column_sum(grad), first)

    @pl.when(first)
    def _():
        dtab_ref[...] = jnp.zeros_like(dtab_ref)

    lang = lang_of(meta, 0, at)
    dtab_ref[pl.ds(lang, 1), :] += column_sum(d_base)


def weight_grad_kernel(table, a0_ref, a1_ref, b0_ref, b1_ref, keep_ref, away_ref, total, *, at):
    step = pl.program_id(0)
    groups, _, cols = total.shape
    value = t_dot(a0_ref[...], b0_ref[...]) + t_dot(a1_ref[...], b1_ref[...])

    @pl.when(step == 0)
    def _():
        for g in range(groups):
            total[g] = value[:, cols * g : cols * g + cols]

    @pl.when(step > 0)
    def _():
        for g in range(groups):
            total[g] += value[:, cols * g : cols * g + cols]

    @pl.when(step == pl.num_programs(0) - 1)
    def _():
        put_pieces(table, at, total, keep_ref, away_ref)


def plus(a, b):
    return (a.astype(F32) + b.astype(F32)).astype(BF16)


def finish_kernel(table, near_ref, far_ref, out_ref, *, at):
    half, rows, cols = near_ref.shape
    groups = out_ref.shape[-1] // cols
    for p in range(2 * half):
        s = table[at + p]
        place = lax.rem(s, half)
        value = jnp.where(
            s < half, near_ref[place].astype(F32), far_ref[place].astype(F32)
        )
        r, g = p // groups, p % groups
        out_ref[rows * r : rows * r + rows, cols * g : cols * g + cols] = value


class Line:
    def __init__(self):
        self.last = None

    def tie(self, *xs):
        if self.last is not None:
            *xs, self.last = lax.optimization_barrier((*xs, self.last))
        return xs

    def call(
        self, kernel, scalars, grid, operands, outs, scratch=(), alias=None, vmem=VMEM, mark=-1
    ):
        arrays, in_specs = zip(*operands)
        shapes, out_specs = zip(*outs)
        (scalars,) = self.tie(scalars)
        results = pl.pallas_call(
            kernel,
            out_shape=shapes,
            grid_spec=pltpu.PrefetchScalarGridSpec(
                num_scalar_prefetch=1,
                grid=grid,
                in_specs=in_specs,
                out_specs=out_specs,
                scratch_shapes=scratch,
            ),
            input_output_aliases=alias or {},
            compiler_params=pltpu.CompilerParams(vmem_limit_bytes=vmem),
            cost_estimate=pl.CostEstimate(flops=1, bytes_accessed=1, transcendentals=0),
        )(scalars, *arrays)
        if mark is not None:
            self.last = results[mark]
        return results


def shaped(shape, dtype):
    return jax.ShapeDtypeStruct(shape, dtype)


def whole(x):
    return (x, pl.BlockSpec(x.shape, lambda i, meta: (0,) * x.ndim, pipeline_mode=pl.Buffered(1)))


def whole_out(shape, dtype):
    return (shaped(shape, dtype), pl.BlockSpec(shape, lambda i, meta: (0,) * len(shape)))


def any_place(x):
    return (x, pl.BlockSpec(memory_space=pl.ANY))


def row_blocks(x, span, first=0):
    lead = x.shape[:-2]
    spec = pl.BlockSpec(
        lead + (span, x.shape[-1]), lambda i, meta: (0,) * len(lead) + (first + i, 0)
    )
    return (x, spec)


def local_blocks(x, span, side):
    return (x, pl.BlockSpec((span, x.shape[-1]), lambda i, meta: (meta[side] + i, 0)))


def item_blocks(x, each=1, first=0):
    lead = (0,) * (x.ndim - 1)
    return (x, pl.BlockSpec((each,) + x.shape[1:], lambda i, meta: (first + i,) + lead))


def swap(x):
    return lax.ppermute(x, "head", [(0, 1), (1, 0)])


class Sums:
    def __init__(self, line, n_dp, n_head):
        self.line, self.n_dp, self.n_head = line, n_dp, n_head
        self.bits = n_dp.bit_length() - 1
        self.pieces = n_dp // 2
        self.me = lax.axis_index("dp")
        self.head = lax.axis_index("head")

    def order(self, *first):
        bits = [b for b in first if b < self.bits]
        bits += [b for b in range(self.bits) if b not in bits]
        swapped = [{0: 1, 1: 0}.get(b, b) if self.bits > 1 else b for b in bits]
        return (tuple(bits), tuple(swapped))

    def static(self, order):
        slots = np.arange(self.pieces)
        rows = []
        for me in range(self.n_dp):
            for h in range(self.n_head):
                cut = sorted(order[h][:-1])
                there = np.zeros(self.pieces, np.int32)
                for s, bit in enumerate(order[h][:-1]):
                    there |= ((slots >> (self.bits - 2 - s)) & 1) << cut.index(bit)
                mine = sum(((me >> bit) & 1) << i for i, bit in enumerate(cut))
                piece_of = there ^ mine
                rows.append(np.concatenate([piece_of, np.argsort(piece_of)]))
        return np.stack(rows).astype(np.int32)

    def prepare(self, orders):
        self.offsets = {order: 2 + 2 * self.pieces * i for i, order in enumerate(orders)}
        every = np.concatenate([self.static(order) for order in orders], axis=1)
        device = self.me * self.n_head + self.head
        return lax.dynamic_slice(jnp.asarray(every), (device, 0), (1, every.shape[1]))[0]

    def piece_at(self, order):
        return self.offsets[order]

    def slot_at(self, order):
        return self.offsets[order] + self.pieces

    def send(self, x, order, stage):
        perm = []
        for d in range(self.n_dp):
            for h in range(self.n_head):
                to = d ^ (1 << order[h][stage])
                perm.append((d * self.n_head + h, to * self.n_head + h))
        return lax.ppermute(x, AXES, perm)

    def piece_shape(self, m, n):
        return (m * n // (self.pieces * 640), 640)

    def halves_out(self, m, n):
        return [whole_out((self.pieces // 2,) + self.piece_shape(m, n), BF16)] * 2

    def weight_grad(self, a0, a1, b0, b1, step, order):
        rows, m = a0[0].shape
        n = b0[0].shape[-1]
        groups = n // 640
        return self.line.call(
            partial(weight_grad_kernel, at=self.piece_at(order)),
            self.scalars,
            (rows // step,),
            [a0, a1, b0, b1],
            self.halves_out(m, n),
            [pltpu.VMEM((groups, m, 640), F32)],
        )

    def reduce(self, keep, away, order, finish):
        for stage in range(self.bits - 1):
            got = self.send(away, order, stage)
            yield
            keep, got = self.line.tie(keep, got)
            half = keep.shape[0] // 2
            if half:
                keep, away = plus(keep[:half], got[:half]), plus(keep[half:], got[half:])
                self.line.last = away
            else:
                keep = plus(keep, got)
                self.line.last = keep
        got = self.send(keep, order, self.bits - 1)
        yield
        keep, got = self.line.tie(keep, got)
        keep = plus(keep, got)
        self.line.last = keep
        for stage in reversed(range(1, self.bits - 1)):
            got = self.send(keep, order, stage)
            yield
            keep, got = self.line.tie(keep, got)
            keep = jnp.concatenate([keep, got], axis=0)
            self.line.last = keep
        got = self.send(keep, order, 0)
        yield
        finish(keep, got)

    def finish(self, near, far, order, shape):
        (result,) = self.line.call(
            partial(finish_kernel, at=self.slot_at(order)),
            self.scalars,
            (1,),
            [whole(near), whole(far)],
            [whole_out(shape, F32)],
            vmem=20 * 2**20,
        )
        return result

    def finish3(self, parts, orders, shape):
        operands = [whole(x) for pair in parts for x in pair]

        def kernel(table, *refs):
            out_ref = refs[-1]
            for c in range(3):

                @pl.when(pl.program_id(0) == c)
                def _(c=c):
                    finish_kernel(
                        table,
                        refs[2 * c],
                        refs[2 * c + 1],
                        out_ref.at[0],
                        at=self.slot_at(orders[c]),
                    )

        spec = pl.BlockSpec((1,) + shape[1:], lambda i, slot: (i, 0, 0))
        (result,) = self.line.call(
            kernel, self.scalars, (3,), operands, [(shaped(shape, F32), spec)], vmem=24 * 2**20
        )
        return result


def sum_small(line, x, total, finish):
    bit = 1
    while bit < total:
        got = lax.ppermute(x, AXES, [(i, i ^ bit) for i in range(total)])
        yield
        x, got = line.tie(x, got)
        x = x + got
        line.last = x
        bit *= 2
    finish(x)


def body(
    latents,
    languages,
    lang_table,
    norm1_gain,
    norm1_shift,
    qkv_weight,
    out_weight,
    out_bias,
    norm2_gain,
    norm2_shift,
    up_weight,
    up_bias,
    down_weight,
    down_bias,
    cotangent,
):
    n_dp, n_head = lax.axis_size("dp"), lax.axis_size("head")
    head = lax.axis_index("head")
    width = latents.shape[1]
    half = width // 2
    heads = half // HEAD_DIM
    span = latents.shape[0] // languages.shape[0]
    rows = latents.shape[0] // 2
    items = rows // span
    line = Line()
    call = line.call
    sums = Sums(line, n_dp, n_head)
    orders = {name: sums.order(*bits) for name, bits in CROSS.items()}
    qkv_orders = tuple(orders[c] for c in range(3))
    starts = jnp.stack([head * items, (1 - head) * items]).astype(jnp.int32)
    tables = sums.prepare(sorted(set(orders.values())))
    scalars = jnp.concatenate([starts, tables, languages.astype(jnp.int32)])
    sums.scalars = scalars
    lang_at = 2 + tables.shape[0]

    qkv = jnp.transpose(qkv_weight, (1, 0, 2))
    wo = (out_weight, swap(out_weight))
    wu = (up_weight, swap(up_weight))
    wd = (down_weight, swap(down_weight))
    ub = (up_bias, swap(up_bias))

    lat = local_blocks(latents, span, 0)
    cot = local_blocks(cotangent, span, 0)
    tab = whole(lang_table)
    gain1, shift1 = whole(norm1_gain), whole(norm1_shift)

    def rows_out(cols, dtype, lead=()):
        shape = shaped(lead + (rows, cols), dtype)
        return (shape, row_blocks(shape, span)[1])

    def sum_out(*shape):
        return whole_out(shape, F32)

    def half_out(shape, spec):
        return (shape, spec)

    grid = (items,)
    h1_shape = shaped((2 * rows, width), BF16)
    proj_shape = shaped((3, 2 * rows, half), BF16)
    prob_shape = shaped((2 * items, heads, span, span), BF16)

    def attend_side(side, into):
        first = side * items
        operands = [local_blocks(latents, span, side), tab, gain1, shift1, whole(qkv)]
        alias = None
        if into is not None:
            operands += [any_place(x) for x in into]
            alias = {1 + 5 + i: i for i in range(3)}

        def kernel(meta, *refs):
            attend_kernel(meta, *refs[:5], *refs[len(operands) :], side=side, at=lang_at)

        return call(
            kernel,
            scalars,
            grid,
            operands,
            [
                row_blocks(h1_shape, span, first),
                row_blocks(proj_shape, span, first),
                item_blocks(prob_shape, 1, first),
                rows_out(half, BF16),
            ],
            alias=alias,
        )

    h1, proj, prob, mixed_p = attend_side(1, None)
    mixed_x = swap(mixed_p)
    h1, proj, prob, mixed_o = attend_side(0, (h1, proj, prob))
    h2, act0, act1, dpre0, dpre1, low, dmix0, dmix1, block_out, *sums2 = call(
        partial(feed_kernel, at=lang_at),
        scalars,
        grid,
        [lat, tab, cot, row_blocks(mixed_o, span), row_blocks(mixed_x, span)]
        + [whole(wo[0]), whole(wo[1]), whole(wd[0]), whole(wd[1]), whole(wu[0]), whole(wu[1])]
        + [whole(ub[0]), whole(ub[1]), whole(out_bias), whole(down_bias)]
        + [whole(norm2_gain), whole(norm2_shift)],
        [rows_out(width, BF16)]
        + [rows_out(half, BF16)] * 4
        + [rows_out(width, BF16), rows_out(half, BF16), rows_out(half, BF16)]
        + [rows_out(width, BF16)]
        + [sum_out(1, width)] * 4
        + [sum_out(1, half)] * 2,
        vmem=58 * 2**20,
        mark=0,
    )
    dgain2, dshift2, dbias, ddownb, dupb0, dupb1 = sums2
    step = min(rows, 512)
    got, grads, results, queue, later = {}, {}, {}, [], []
    shapes = {"down": down_weight.shape, "up": up_weight.shape, "out": out_weight.shape}

    def shared(x, side):
        return (
            x,
            pl.BlockSpec(
                (step, x.shape[-1]), lambda i, s: (s[side] * span // step + i, 0)
            ),
        )

    def blocks(x):
        return row_blocks(x, step)

    def trade(**arrays):
        for name, x in arrays.items():
            if isinstance(x, (list, tuple)):
                got[name] = [swap(piece) for piece in line.tie(*x)]
            else:
                (x,) = line.tie(x)
                got[name] = swap(x)

    def begin(chain):
        next(chain)
        queue.append(chain)

    def advance():
        if queue:
            chain = queue.pop(0)
            if next(chain, "end") != "end":
                queue.append(chain)

    def keep_result(name, order):
        def finish(near, far):
            later.append((name, near, far, order))

        return finish

    def do_finish():
        if later:
            name, near, far, order = later.pop(0)
            results[name] = sums.finish(near, far, order, shapes[name])

    def keep_parts(c):
        def finish(near, far):
            grads[c] = (near, far)

        return finish

    def weight(name, order, *operands):
        keep, away = sums.weight_grad(*operands, step, order)
        begin(sums.reduce(keep, away, order, keep_result(name, order)))

    def do_down():
        operands = [blocks(act0), blocks(got["act"]), shared(cotangent, 0), shared(cotangent, 1)]
        weight("down", orders["down"], *operands)

    def do_up():
        weight("up", orders["up"], blocks(h2), blocks(got["h2"]), blocks(dpre0), blocks(got["dpre"]))

    def do_out():
        weight("out", orders["out"], blocks(mixed_o), blocks(mixed_p), blocks(low), blocks(got["low"]))

    each = 2 if items % 2 == 0 else 1
    count = items // each
    wide = each * span

    def do_attend():
        dproj_shape = shaped((3, 2 * rows, half), BF16)
        dmix_own = pl.BlockSpec((wide, half), lambda i, s: (jnp.minimum(i, count - 1), 0))
        dmix_other = pl.BlockSpec((wide, half), lambda i, s: (jnp.maximum(i - count, 0), 0))
        grads["dproj"], *pieces = call(
            partial(
                attend_back_kernel,
                items=items,
                each=each,
                at=[sums.piece_at(order) for order in qkv_orders],
            ),
            scalars,
            (2 * count,),
            [row_blocks(h1, wide), row_blocks(proj, wide), item_blocks(prob, each)]
            + [(dmix0, dmix_own), (got["dmix"], dmix_other)],
            [row_blocks(dproj_shape, wide)] + sums.halves_out(width, half) * 3,
            [pltpu.VMEM((3, width, half), F32)],
            vmem=50 * 2**20,
            mark=0,
        )
        for c in SENDS:
            begin(sums.reduce(pieces[2 * c], pieces[2 * c + 1], qkv_orders[c], keep_parts(c)))

    def do_part():
        grads["part"] = call(
            hidden_grad_kernel,
            scalars,
            grid,
            [row_blocks(grads["dproj"], span, items), whole(qkv)],
            [whole_out((span, width), BF16)] * items,
            vmem=30 * 2**20,
        )

    def do_base():
        dbase, dgain1, dshift1, dtab = call(
            partial(base_grad_kernel, at=lang_at),
            scalars,
            grid,
            [whole(x) for x in got["part"]]
            + [lat, tab, row_blocks(low, span), row_blocks(grads["dproj"], span), whole(qkv), gain1],
            [rows_out(width, F32), sum_out(1, width), sum_out(1, width)]
            + [sum_out(*lang_table.shape)],
            vmem=30 * 2**20,
        )
        results["dbase"] = dbase
        dupb = jnp.where(
            head == 0,
            jnp.concatenate([dupb0, dupb1], axis=1),
            jnp.concatenate([dupb1, dupb0], axis=1),
        )
        small = [dtab, dgain1, dshift1, dbias, dgain2, dshift2, ddownb, dupb]
        begin(
            sum_small(
                line,
                jnp.concatenate(small, axis=0),
                n_dp * n_head,
                lambda x: results.update(small=x),
            )
        )

    def do_qkv():
        results["qkv"] = sums.finish3([grads[c] for c in range(3)], qkv_orders, qkv.shape)

    kernels = {
        "WD": do_down,
        "WU": do_up,
        "WO": do_out,
        "B": do_attend,
        "F": do_finish,
        "H1": do_part,
        "H2": do_base,
        "T1": lambda: trade(act=act1, dmix=dmix1, dpre=dpre1, h2=h2),
        "T2": lambda: trade(low=low),
        "T3": lambda: trade(part=grads["part"]),
    }
    for word in STEPS:
        if word in kernels:
            kernels[word]()
        else:
            for _ in range(word):
                advance()
    while queue:
        advance()
    while later:
        do_finish()
    do_qkv()
    small = results["small"]
    langs = lang_table.shape[0]
    dgain1, dshift1, dbias, dgain2, dshift2, ddownb, dupb = [small[langs + i] for i in range(7)]
    dupb = lax.dynamic_slice_in_dim(dupb, head * half, half, 0)
    return (
        block_out,
        results["dbase"],
        small[:langs],
        dgain1,
        dshift1,
        jnp.transpose(results["qkv"], (1, 0, 2)),
        results["out"],
        dbias,
        dgain2,
        dshift2,
        results["up"],
        dupb,
        results["down"],
        ddownb,
    )


def normalize(values, gain, shift):
    mean = jnp.mean(values, axis=-1, keepdims=True)
    centred = values - mean
    inverse = lax.rsqrt(jnp.mean(centred * centred, axis=-1, keepdims=True) + EPS)
    unit = centred * inverse
    return (unit * gain + shift, unit, inverse)


def normalize_back(grad, unit, inverse, gain):
    scaled = grad * gain
    return inverse * (
        scaled
        - jnp.mean(scaled, axis=-1, keepdims=True)
        - unit * jnp.mean(scaled * unit, axis=-1, keepdims=True)
    )


def own_rows(values, start, share):
    return lax.dynamic_slice_in_dim(values, start, share, 0)


def plain_body(
    latents,
    languages,
    lang_table,
    norm1_gain,
    norm1_shift,
    qkv_weight,
    out_weight,
    out_bias,
    norm2_gain,
    norm2_shift,
    up_weight,
    up_bias,
    down_weight,
    down_bias,
    cotangent,
):
    f32 = jnp.float32
    bf16 = jnp.bfloat16
    items = languages.shape[0]
    rows = latents.shape[0]
    span = rows // items
    width = latents.shape[1]
    local = qkv_weight.shape[2]
    heads_here = local // HEAD_DIM
    scale = HEAD_DIM ** (-0.5)
    share = rows // lax.axis_size("head")
    start = lax.axis_index("head") * share
    token_lang = jnp.repeat(languages, span)
    onehot = (
        token_lang[:, None] == jnp.arange(lang_table.shape[0], dtype=jnp.int32)[None, :]
    ).astype(bf16)
    base = latents.astype(f32) + jnp.dot(onehot, lang_table, preferred_element_type=f32)
    normed1, unit1, inverse1 = normalize(base, norm1_gain, norm1_shift)
    h_one = normed1.astype(bf16)
    qkv_flat = qkv_weight.reshape(width, 3 * local)
    proj = jnp.dot(h_one, qkv_flat, preferred_element_type=f32).astype(bf16)
    proj = proj.reshape(items, span, 3, heads_here, HEAD_DIM)
    query = proj[:, :, 0]
    key = proj[:, :, 1]
    value = proj[:, :, 2]
    raw = jnp.einsum("iqhd,ikhd->ihqk", query, key, preferred_element_type=f32) * scale
    peak = jnp.max(raw, axis=-1, keepdims=True)
    weights = jnp.exp(raw - peak)
    probs = weights / jnp.sum(weights, axis=-1, keepdims=True)
    probs_low = probs.astype(bf16)
    mixed = jnp.einsum("ihqk,ikhd->iqhd", probs_low, value, preferred_element_type=f32)
    mixed = mixed.astype(bf16).reshape(rows, local)
    attn_part = jnp.dot(mixed, out_weight, preferred_element_type=f32)
    attn_full = lax.psum(attn_part, "head")
    middle = base + attn_full + out_bias
    normed2, unit2, inverse2 = normalize(middle, norm2_gain, norm2_shift)
    h_two = normed2.astype(bf16)
    pre = jnp.dot(h_two, up_weight, preferred_element_type=f32) + up_bias
    act, gelu_back = jax.vjp(partial(jax.nn.gelu, approximate=True), pre)
    act_low = act.astype(bf16)
    down_part = jnp.dot(act_low, down_weight, preferred_element_type=f32)
    final = (
        middle + lax.psum(down_part.astype(jnp.bfloat16), "head").astype(jnp.float32) + down_bias
    )
    block_out = own_rows(final, start, share).astype(bf16)
    grad_rows = cotangent.astype(f32)
    d_act = jnp.einsum("td,fd->tf", cotangent, down_weight, preferred_element_type=f32)
    d_down = jnp.einsum("tf,td->fd", act_low, cotangent, preferred_element_type=f32)
    d_pre_low = gelu_back(d_act)[0].astype(bf16)
    d_up = jnp.einsum("td,tf->df", h_two, d_pre_low, preferred_element_type=f32)
    d_up_bias = jnp.sum(d_pre_low.astype(f32), axis=0)
    h2_part = jnp.einsum("tf,df->td", d_pre_low, up_weight, preferred_element_type=f32)
    h2_grad = lax.psum(h2_part, "head")
    d_middle = grad_rows + normalize_back(h2_grad, unit2, inverse2, norm2_gain)
    d_middle_low = d_middle.astype(bf16)
    d_gain2 = jnp.sum(h2_grad * unit2, axis=0)
    d_shift2 = jnp.sum(h2_grad, axis=0)
    d_out_bias = jnp.sum(d_middle, axis=0)
    d_down_bias = jnp.sum(grad_rows, axis=0)
    d_out = jnp.einsum("tc,td->cd", mixed, d_middle_low, preferred_element_type=f32)
    d_mixed = jnp.einsum("td,cd->tc", d_middle_low, out_weight, preferred_element_type=f32)
    d_mixed = d_mixed.astype(bf16).reshape(items, span, heads_here, HEAD_DIM)
    d_probs = jnp.einsum("iqhd,ikhd->ihqk", d_mixed, value, preferred_element_type=f32)
    d_value = jnp.einsum("ihqk,iqhd->ikhd", probs_low, d_mixed, preferred_element_type=f32)
    d_raw = probs * (d_probs - jnp.sum(probs * d_probs, axis=-1, keepdims=True))
    d_raw_low = d_raw.astype(bf16)
    d_query = jnp.einsum("ihqk,ikhd->iqhd", d_raw_low, key, preferred_element_type=f32) * scale
    d_key = jnp.einsum("ihqk,iqhd->ikhd", d_raw_low, query, preferred_element_type=f32) * scale
    d_proj = jnp.stack([d_query, d_key, d_value], axis=2).astype(bf16).reshape(rows, 3 * local)
    d_qkv = jnp.einsum("td,tc->dc", h_one, d_proj, preferred_element_type=f32).reshape(
        width, 3, local
    )
    h1_part = jnp.einsum("tc,dc->td", d_proj, qkv_flat, preferred_element_type=f32)
    h1_grad = lax.psum(h1_part.astype(jnp.bfloat16), "head").astype(jnp.float32)
    d_base = d_middle + normalize_back(h1_grad, unit1, inverse1, norm1_gain)
    onehot_own = onehot.astype(f32)
    input_grad = own_rows(d_base, start, share)
    d_gain1 = jnp.sum(h1_grad * unit1, axis=0)
    d_shift1 = jnp.sum(h1_grad, axis=0)
    d_table = jnp.einsum("tl,td->ld", onehot_own, d_base, precision=HIGH)
    (
        d_qkv,
        d_out,
        d_up,
        d_up_bias,
        d_down,
        d_table,
        d_gain1,
        d_shift1,
        d_out_bias,
        d_gain2,
        d_shift2,
        d_down_bias,
    ) = (
        lax.psum(d_qkv.astype(jnp.bfloat16), "dp").astype(jnp.float32),
        lax.psum(d_out.astype(jnp.bfloat16), "dp").astype(jnp.float32),
        lax.psum(d_up.astype(jnp.bfloat16), "dp").astype(jnp.float32),
        lax.psum(d_up_bias.astype(jnp.bfloat16), "dp").astype(jnp.float32),
        lax.psum(d_down.astype(jnp.bfloat16), "dp").astype(jnp.float32),
        lax.psum(d_table.astype(jnp.bfloat16), "dp").astype(jnp.float32),
        lax.psum(d_gain1.astype(jnp.bfloat16), "dp").astype(jnp.float32),
        lax.psum(d_shift1.astype(jnp.bfloat16), "dp").astype(jnp.float32),
        lax.psum(d_out_bias.astype(jnp.bfloat16), "dp").astype(jnp.float32),
        lax.psum(d_gain2.astype(jnp.bfloat16), "dp").astype(jnp.float32),
        lax.psum(d_shift2.astype(jnp.bfloat16), "dp").astype(jnp.float32),
        lax.psum(d_down_bias.astype(jnp.bfloat16), "dp").astype(jnp.float32),
    )
    return (
        block_out,
        input_grad,
        d_table,
        d_gain1,
        d_shift1,
        d_qkv,
        d_out,
        d_out_bias,
        d_gain2,
        d_shift2,
        d_up,
        d_up_bias,
        d_down,
        d_down_bias,
    )


def solution(mesh):
    in_specs = (
        P("dp", None),
        P("dp"),
        P(),
        P(),
        P(),
        P(None, None, "head"),
        P("head", None),
        P(),
        P(),
        P(),
        P(None, "head"),
        P("head"),
        P("head", None),
        P(),
        P("dp", None),
    )
    out_specs = (
        P(("dp", "head"), None),
        P(("dp", "head"), None),
        P(),
        P(),
        P(),
        P(None, None, "head"),
        P("head", None),
        P(),
        P(),
        P(),
        P(None, "head"),
        P("head"),
        P("head", None),
        P(),
    )
    return jax.shard_map(
        body if mesh.shape["head"] == 2 else plain_body,
         mesh=mesh, in_specs=in_specs, out_specs=out_specs, check_vma=False)
```

```python
from functools import partial

import numpy as np

import jax
import jax.numpy as jnp
from jax import lax
from jax.experimental import pallas as pl
from jax.experimental.pallas import tpu as pltpu
from jax.sharding import PartitionSpec as P

HEAD_DIM = 160
EPS = 1e-05
SCALE = HEAD_DIM ** (-0.5)
LANE = 128
WINDOW = 256
VMEM = 60 * 2**20
F32 = jnp.float32
BF16 = jnp.bfloat16
AXES = ("dp", "head")
HIGH = lax.Precision.HIGHEST
ROOT = 0.7978845608028654
CUBE = 0.044715


def dot(a, b):
    return jnp.dot(a, b, preferred_element_type=F32)


def dot_t(a, b):
    return lax.dot_general(a, b, (((1,), (1,)), ((), ())), preferred_element_type=F32)


def t_dot(a, b):
    return lax.dot_general(a, b, (((0,), (0,)), ((), ())), preferred_element_type=F32)


def row_mean(v):
    return jnp.mean(v, axis=-1, keepdims=True)


def unit_of(v):
    centred = v - row_mean(v)
    inverse = lax.rsqrt(row_mean(centred * centred) + EPS)
    return centred * inverse, inverse


def unit_back(grad, unit, inverse, gain):
    scaled = grad * gain
    return inverse * (scaled - row_mean(scaled) - unit * row_mean(scaled * unit))


def column_sum(v):
    return jnp.sum(v, axis=0, keepdims=True)


def line_of(ref):
    return ref[...].reshape(1, -1)


def add_to(ref, value, first):
    @pl.when(first)
    def _():
        ref[...] = value

    @pl.when(jnp.logical_not(first))
    def _():
        ref[...] += value


def table_row(tab_ref, lang):
    table = tab_ref[...].astype(F32)
    rows = lax.broadcasted_iota(jnp.int32, table.shape, 0)
    return jnp.sum(jnp.where(rows == lang, table, 0.0), axis=0, keepdims=True)


def lang_of(meta, side, at):
    return meta[at + meta[side] + pl.program_id(0)]


def base_of(meta, lat_ref, tab_ref, side, at):
    return lat_ref[...].astype(F32) + table_row(tab_ref, lang_of(meta, side, at))


def head_mask(a):
    lane = lax.broadcasted_iota(jnp.int32, (1, WINDOW), 1)
    first = HEAD_DIM * a - LANE * a
    return ((lane >= first) & (lane < first + HEAD_DIM)).astype(F32).astype(BF16)


def join_heads(parts):
    lane = lax.broadcasted_iota(jnp.int32, (parts[0].shape[0], LANE), 1)
    blocks = [parts[0][:, :LANE]]
    for b in range(1, len(parts)):
        edge = HEAD_DIM * b - LANE * b
        blocks.append(jnp.where(lane < edge, parts[b - 1][:, LANE:], parts[b][:, :LANE]))
    blocks.append(parts[-1][:, LANE:])
    return jnp.concatenate(blocks, axis=1)


def windows(count):
    return [slice(LANE * a, LANE * a + WINDOW) for a in range(count)]


STEPS = ("T1", "WD", "T2", 0, "WU", 1, "WO", 2, "B", 1, "H1", 2, "T3", 4, "H2", 33, "F", "F", "F")
SENDS = (0, 1, 2)
CROSS = {"down": (0, 2, 1, 3), "up": (0, 1, 2, 3), "out": (2, 0, 1, 3), 0: (0, 2, 1, 3), 1: (0, 1, 2, 3), 2: (2, 0, 1, 3)}


def attend_kernel(
    meta,
    lat_ref,
    tab_ref,
    gain_ref,
    shift_ref,
    w_ref,
    h_ref,
    proj_ref,
    prob_ref,
    mixed_ref,
    *,
    side,
    at,
):
    unit, _ = unit_of(base_of(meta, lat_ref, tab_ref, side, at))
    hidden = (unit * line_of(gain_ref) + line_of(shift_ref)).astype(BF16)
    h_ref[...] = hidden
    for c in range(3):
        proj_ref[c] = dot(hidden, w_ref[c]).astype(BF16)
    lanes = windows(prob_ref.shape[1])
    raw = [
        dot_t(proj_ref[0, :, w] * head_mask(a), proj_ref[1, :, w]) for a, w in enumerate(lanes)
    ]
    low = []
    for a, scores in enumerate(raw):
        scores = scores * SCALE
        weights = jnp.exp(scores - jnp.max(scores, axis=-1, keepdims=True))
        probs = weights * (1.0 / jnp.sum(weights, axis=-1, keepdims=True))
        low.append(probs.astype(BF16))
        prob_ref[0, a] = low[a]
    parts = [dot(low[a], proj_ref[2, :, w]) for a, w in enumerate(lanes)]
    mixed_ref[...] = join_heads(parts).astype(BF16)


def gelu(x):
    square = x * x
    tanh = jnp.tanh(x * (ROOT + (ROOT * CUBE) * square))
    half = 0.5 + 0.5 * tanh
    slope = half + x * (1.0 - tanh * tanh) * (0.5 * ROOT + (1.5 * ROOT * CUBE) * square)
    return x * half, slope


def feed_kernel(
    meta,
    lat_ref,
    tab_ref,
    cot_ref,
    mix0_ref,
    mix1_ref,
    out0_ref,
    out1_ref,
    down0_ref,
    down1_ref,
    up0_ref,
    up1_ref,
    upb0_ref,
    upb1_ref,
    outb_ref,
    downb_ref,
    gain_ref,
    shift_ref,
    h_ref,
    act0_ref,
    act1_ref,
    dpre0_ref,
    dpre1_ref,
    low_ref,
    dmix0_ref,
    dmix1_ref,
    block_ref,
    dgain_ref,
    dshift_ref,
    doutb_ref,
    ddownb_ref,
    dupb0_ref,
    dupb1_ref,
    *,
    at,
):
    first = pl.program_id(0) == 0
    base = base_of(meta, lat_ref, tab_ref, 0, at)
    attn = dot(mix0_ref[...], out0_ref[...]) + dot(mix1_ref[...], out1_ref[...])
    middle = base + attn + line_of(outb_ref)
    cot = cot_ref[...]
    d_act = (dot_t(cot, down0_ref[...]), dot_t(cot, down1_ref[...]))
    unit, inverse = unit_of(middle)
    hidden = (unit * line_of(gain_ref) + line_of(shift_ref)).astype(BF16)
    h_ref[...] = hidden
    pre = (dot(hidden, up0_ref[...]) + line_of(upb0_ref), dot(hidden, up1_ref[...]) + line_of(upb1_ref))
    acts, d_pres = [], []
    for j, (act_ref, dpre_ref, dupb_ref) in enumerate(
        ((act0_ref, dpre0_ref, dupb0_ref), (act1_ref, dpre1_ref, dupb1_ref))
    ):
        act, slope = gelu(pre[j])
        acts.append(act.astype(BF16))
        d_pres.append((d_act[j] * slope).astype(BF16))
        act_ref[...] = acts[j]
        dpre_ref[...] = d_pres[j]
        add_to(dupb_ref, column_sum(d_pres[j].astype(F32)), first)
    grad = dot_t(d_pres[0], up0_ref[...]) + dot_t(d_pres[1], up1_ref[...])
    out = dot(acts[0], down0_ref[...]) + dot(acts[1], down1_ref[...])
    block_ref[...] = (middle + out + line_of(downb_ref)).astype(BF16)
    cot = cot.astype(F32)
    d_mid = cot + unit_back(grad, unit, inverse, line_of(gain_ref))
    low = d_mid.astype(BF16)
    low_ref[...] = low
    dmix1_ref[...] = dot_t(low, out1_ref[...]).astype(BF16)
    dmix0_ref[...] = dot_t(low, out0_ref[...]).astype(BF16)
    add_to(dgain_ref, column_sum(grad * unit), first)
    add_to(dshift_ref, column_sum(grad), first)
    add_to(doutb_ref, column_sum(d_mid), first)
    add_to(ddownb_ref, column_sum(cot), first)


def put_pieces(table, at, total, keep_ref, away_ref):
    half, rows = keep_ref.shape[-3:-1]
    groups = total.shape[0]
    for s in range(half):
        for ref, slot in ((keep_ref, s), (away_ref, s + half)):
            p = table[at + slot]
            start = pl.multiple_of(rows * (p // groups), 8)
            ref[s] = total[p % groups, pl.ds(start, rows), :].astype(BF16)


def attend_back_kernel(
    table,
    h_ref,
    proj_ref,
    prob_ref,
    dmixo_ref,
    dmixp_ref,
    dproj_ref,
    *rest,
    items,
    each,
    at,
):
    outs, total = rest[:6], rest[6]
    step = pl.program_id(0)
    last = 2 * items // each - 1
    own = step < items // each
    span = proj_ref.shape[1] // each
    d_all = jnp.where(own, dmixo_ref[...], dmixp_ref[...])
    lanes = windows(prob_ref.shape[1])
    for u in range(each):
        rows = slice(span * u, span * u + span)
        d_mixed = [d_all[rows, w] for w in lanes]
        low = [prob_ref[u, a] for a in range(len(lanes))]
        d_probs = [
            dot_t(d_mixed[a] * head_mask(a), proj_ref[2, rows, w]) for a, w in enumerate(lanes)
        ]
        d_value = [t_dot(low[a], d_mixed[a]) for a in range(len(lanes))]
        d_low = []
        for a in range(len(lanes)):
            probs = low[a].astype(F32)
            d_raw = probs * (d_probs[a] - jnp.sum(probs * d_probs[a], axis=-1, keepdims=True))
            d_low.append(d_raw.astype(BF16))
        d_query = [dot(d_low[a], proj_ref[1, rows, w]) * SCALE for a, w in enumerate(lanes)]
        d_key = [t_dot(d_low[a], proj_ref[0, rows, w]) * SCALE for a, w in enumerate(lanes)]
        for c, parts in enumerate((d_query, d_key, d_value)):
            dproj_ref[c, rows] = join_heads(parts).astype(BF16)

    @pl.when(step == 0)
    def _():
        for c in range(3):
            total[c] = t_dot(h_ref[...], dproj_ref[c])

    @pl.when(step > 0)
    def _():
        for c in range(3):
            total[c] += t_dot(h_ref[...], dproj_ref[c])

    @pl.when(step == last)
    def _():
        for c in range(3):
            put_pieces(table, at[c], total.at[c : c + 1], outs[2 * c], outs[2 * c + 1])


def hidden_grad_kernel(meta, dproj_ref, w_ref, *out_refs):
    grad = dot_t(dproj_ref[0], w_ref[0])
    for c in range(1, 3):
        grad += dot_t(dproj_ref[c], w_ref[c])
    for i, out_ref in enumerate(out_refs):

        @pl.when(pl.program_id(0) == i)
        def _(out_ref=out_ref):
            out_ref[...] = grad.astype(BF16)


def base_grad_kernel(meta, *refs, at):
    part_refs = refs[:-10]
    lat_ref, tab_ref, low_ref, dproj_ref, w_ref, gain_ref = refs[-10:-4]
    dbase_ref, dgain_ref, dshift_ref, dtab_ref = refs[-4:]
    first = pl.program_id(0) == 0
    part = part_refs[0][...]
    for i in range(1, len(part_refs)):
        part = jnp.where(pl.program_id(0) == i, part_refs[i][...], part)
    grad = part.astype(F32)
    for c in range(3):
        grad += dot_t(dproj_ref[c], w_ref[c])
    unit, inverse = unit_of(base_of(meta, lat_ref, tab_ref, 0, at))
    d_base = low_ref[...].astype(F32) + unit_back(grad, unit, inverse, line_of(gain_ref))
    dbase_ref[...] = d_base
    add_to(dgain_ref, column_sum(grad * unit), first)
    add_to(dshift_ref, column_sum(grad), first)

    @pl.when(first)
    def _():
        dtab_ref[...] = jnp.zeros_like(dtab_ref)

    lang = lang_of(meta, 0, at)
    dtab_ref[pl.ds(lang, 1), :] += column_sum(d_base)


def weight_grad_kernel(table, a0_ref, a1_ref, b0_ref, b1_ref, keep_ref, away_ref, total, *, at):
    step = pl.program_id(0)
    groups, _, cols = total.shape
    value = t_dot(a0_ref[...], b0_ref[...]) + t_dot(a1_ref[...], b1_ref[...])

    @pl.when(step == 0)
    def _():
        for g in range(groups):
            total[g] = value[:, cols * g : cols * g + cols]

    @pl.when(step > 0)
    def _():
        for g in range(groups):
            total[g] += value[:, cols * g : cols * g + cols]

    @pl.when(step == pl.num_programs(0) - 1)
    def _():
        put_pieces(table, at, total, keep_ref, away_ref)


def plus(a, b):
    return (a.astype(F32) + b.astype(F32)).astype(BF16)


def finish_kernel(table, near_ref, far_ref, out_ref, *, at):
    half, rows, cols = near_ref.shape
    groups = out_ref.shape[-1] // cols
    for p in range(2 * half):
        s = table[at + p]
        place = lax.rem(s, half)
        value = jnp.where(
            s < half, near_ref[place].astype(F32), far_ref[place].astype(F32)
        )
        r, g = p // groups, p % groups
        out_ref[rows * r : rows * r + rows, cols * g : cols * g + cols] = value


class Line:
    def __init__(self):
        self.last = None

    def tie(self, *xs):
        if self.last is not None:
            *xs, self.last = lax.optimization_barrier((*xs, self.last))
        return xs

    def call(
        self, kernel, scalars, grid, operands, outs, scratch=(), alias=None, vmem=VMEM, mark=-1
    ):
        arrays, in_specs = zip(*operands)
        shapes, out_specs = zip(*outs)
        (scalars,) = self.tie(scalars)
        results = pl.pallas_call(
            kernel,
            out_shape=shapes,
            grid_spec=pltpu.PrefetchScalarGridSpec(
                num_scalar_prefetch=1,
                grid=grid,
                in_specs=in_specs,
                out_specs=out_specs,
                scratch_shapes=scratch,
            ),
            input_output_aliases=alias or {},
            compiler_params=pltpu.CompilerParams(vmem_limit_bytes=vmem),
            cost_estimate=pl.CostEstimate(flops=1, bytes_accessed=1, transcendentals=0),
        )(scalars, *arrays)
        if mark is not None:
            self.last = results[mark]
        return results


def shaped(shape, dtype):
    return jax.ShapeDtypeStruct(shape, dtype)


def whole(x):
    return (x, pl.BlockSpec(x.shape, lambda i, meta: (0,) * x.ndim, pipeline_mode=pl.Buffered(1)))


def whole_out(shape, dtype):
    return (shaped(shape, dtype), pl.BlockSpec(shape, lambda i, meta: (0,) * len(shape)))


def any_place(x):
    return (x, pl.BlockSpec(memory_space=pl.ANY))


def row_blocks(x, span, first=0):
    lead = x.shape[:-2]
    spec = pl.BlockSpec(
        lead + (span, x.shape[-1]), lambda i, meta: (0,) * len(lead) + (first + i, 0)
    )
    return (x, spec)


def local_blocks(x, span, side):
    return (x, pl.BlockSpec((span, x.shape[-1]), lambda i, meta: (meta[side] + i, 0)))


def item_blocks(x, each=1, first=0):
    lead = (0,) * (x.ndim - 1)
    return (x, pl.BlockSpec((each,) + x.shape[1:], lambda i, meta: (first + i,) + lead))


def swap(x):
    return lax.ppermute(x, "head", [(0, 1), (1, 0)])


class Sums:
    def __init__(self, line, n_dp, n_head):
        self.line, self.n_dp, self.n_head = line, n_dp, n_head
        self.bits = n_dp.bit_length() - 1
        self.pieces = n_dp // 2
        self.me = lax.axis_index("dp")
        self.head = lax.axis_index("head")

    def order(self, *first):
        bits = [b for b in first if b < self.bits]
        bits += [b for b in range(self.bits) if b not in bits]
        swapped = [{0: 1, 1: 0}.get(b, b) if self.bits > 1 else b for b in bits]
        return (tuple(bits), tuple(swapped))

    def static(self, order):
        slots = np.arange(self.pieces)
        rows = []
        for me in range(self.n_dp):
            for h in range(self.n_head):
                cut = sorted(order[h][:-1])
                there = np.zeros(self.pieces, np.int32)
                for s, bit in enumerate(order[h][:-1]):
                    there |= ((slots >> (self.bits - 2 - s)) & 1) << cut.index(bit)
                mine = sum(((me >> bit) & 1) << i for i, bit in enumerate(cut))
                piece_of = there ^ mine
                rows.append(np.concatenate([piece_of, np.argsort(piece_of)]))
        return np.stack(rows).astype(np.int32)

    def prepare(self, orders):
        self.offsets = {order: 2 + 2 * self.pieces * i for i, order in enumerate(orders)}
        every = np.concatenate([self.static(order) for order in orders], axis=1)
        device = self.me * self.n_head + self.head
        return lax.dynamic_slice(jnp.asarray(every), (device, 0), (1, every.shape[1]))[0]

    def piece_at(self, order):
        return self.offsets[order]

    def slot_at(self, order):
        return self.offsets[order] + self.pieces

    def send(self, x, order, stage):
        perm = []
        for d in range(self.n_dp):
            for h in range(self.n_head):
                to = d ^ (1 << order[h][stage])
                perm.append((d * self.n_head + h, to * self.n_head + h))
        return lax.ppermute(x, AXES, perm)

    def piece_shape(self, m, n):
        return (m * n // (self.pieces * 640), 640)

    def halves_out(self, m, n):
        return [whole_out((self.pieces // 2,) + self.piece_shape(m, n), BF16)] * 2

    def weight_grad(self, a0, a1, b0, b1, step, order):
        rows, m = a0[0].shape
        n = b0[0].shape[-1]
        groups = n // 640
        return self.line.call(
            partial(weight_grad_kernel, at=self.piece_at(order)),
            self.scalars,
            (rows // step,),
            [a0, a1, b0, b1],
            self.halves_out(m, n),
            [pltpu.VMEM((groups, m, 640), F32)],
        )

    def reduce(self, keep, away, order, finish):
        for stage in range(self.bits - 1):
            got = self.send(away, order, stage)
            yield
            keep, got = self.line.tie(keep, got)
            half = keep.shape[0] // 2
            if half:
                keep, away = plus(keep[:half], got[:half]), plus(keep[half:], got[half:])
                self.line.last = away
            else:
                keep = plus(keep, got)
                self.line.last = keep
        got = self.send(keep, order, self.bits - 1)
        yield
        keep, got = self.line.tie(keep, got)
        keep = plus(keep, got)
        self.line.last = keep
        for stage in reversed(range(1, self.bits - 1)):
            got = self.send(keep, order, stage)
            yield
            keep, got = self.line.tie(keep, got)
            keep = jnp.concatenate([keep, got], axis=0)
            self.line.last = keep
        got = self.send(keep, order, 0)
        yield
        finish(keep, got)

    def finish(self, near, far, order, shape):
        (result,) = self.line.call(
            partial(finish_kernel, at=self.slot_at(order)),
            self.scalars,
            (1,),
            [whole(near), whole(far)],
            [whole_out(shape, F32)],
            vmem=20 * 2**20,
        )
        return result

    def finish3(self, parts, orders, shape):
        operands = [whole(x) for pair in parts for x in pair]

        def kernel(table, *refs):
            out_ref = refs[-1]
            for c in range(3):

                @pl.when(pl.program_id(0) == c)
                def _(c=c):
                    finish_kernel(
                        table,
                        refs[2 * c],
                        refs[2 * c + 1],
                        out_ref.at[0],
                        at=self.slot_at(orders[c]),
                    )

        spec = pl.BlockSpec((1,) + shape[1:], lambda i, slot: (i, 0, 0))
        (result,) = self.line.call(
            kernel, self.scalars, (3,), operands, [(shaped(shape, F32), spec)], vmem=24 * 2**20
        )
        return result


def sum_small(line, x, total, finish):
    bit = 1
    while bit < total:
        got = lax.ppermute(x, AXES, [(i, i ^ bit) for i in range(total)])
        yield
        x, got = line.tie(x, got)
        x = x + got
        line.last = x
        bit *= 2
    finish(x)


def body(
    latents,
    languages,
    lang_table,
    norm1_gain,
    norm1_shift,
    qkv_weight,
    out_weight,
    out_bias,
    norm2_gain,
    norm2_shift,
    up_weight,
    up_bias,
    down_weight,
    down_bias,
    cotangent,
):
    n_dp, n_head = lax.axis_size("dp"), lax.axis_size("head")
    head = lax.axis_index("head")
    width = latents.shape[1]
    half = width // 2
    heads = half // HEAD_DIM
    span = latents.shape[0] // languages.shape[0]
    rows = latents.shape[0] // 2
    items = rows // span
    line = Line()
    call = line.call
    sums = Sums(line, n_dp, n_head)
    orders = {name: sums.order(*bits) for name, bits in CROSS.items()}
    qkv_orders = tuple(orders[c] for c in range(3))
    starts = jnp.stack([head * items, (1 - head) * items]).astype(jnp.int32)
    tables = sums.prepare(sorted(set(orders.values())))
    scalars = jnp.concatenate([starts, tables, languages.astype(jnp.int32)])
    sums.scalars = scalars
    lang_at = 2 + tables.shape[0]

    qkv = jnp.transpose(qkv_weight, (1, 0, 2))
    wo = (out_weight, swap(out_weight))
    wu = (up_weight, swap(up_weight))
    wd = (down_weight, swap(down_weight))
    ub = (up_bias, swap(up_bias))

    lat = local_blocks(latents, span, 0)
    cot = local_blocks(cotangent, span, 0)
    tab = whole(lang_table)
    gain1, shift1 = whole(norm1_gain), whole(norm1_shift)

    def rows_out(cols, dtype, lead=()):
        shape = shaped(lead + (rows, cols), dtype)
        return (shape, row_blocks(shape, span)[1])

    def sum_out(*shape):
        return whole_out(shape, F32)

    def half_out(shape, spec):
        return (shape, spec)

    grid = (items,)
    h1_shape = shaped((2 * rows, width), BF16)
    proj_shape = shaped((3, 2 * rows, half), BF16)
    prob_shape = shaped((2 * items, heads, span, span), BF16)

    def attend_side(side, into):
        first = side * items
        operands = [local_blocks(latents, span, side), tab, gain1, shift1, whole(qkv)]
        alias = None
        if into is not None:
            operands += [any_place(x) for x in into]
            alias = {1 + 5 + i: i for i in range(3)}

        def kernel(meta, *refs):
            attend_kernel(meta, *refs[:5], *refs[len(operands) :], side=side, at=lang_at)

        return call(
            kernel,
            scalars,
            grid,
            operands,
            [
                row_blocks(h1_shape, span, first),
                row_blocks(proj_shape, span, first),
                item_blocks(prob_shape, 1, first),
                rows_out(half, BF16),
            ],
            alias=alias,
        )

    h1, proj, prob, mixed_p = attend_side(1, None)
    mixed_x = swap(mixed_p)
    h1, proj, prob, mixed_o = attend_side(0, (h1, proj, prob))
    h2, act0, act1, dpre0, dpre1, low, dmix0, dmix1, block_out, *sums2 = call(
        partial(feed_kernel, at=lang_at),
        scalars,
        grid,
        [lat, tab, cot, row_blocks(mixed_o, span), row_blocks(mixed_x, span)]
        + [whole(wo[0]), whole(wo[1]), whole(wd[0]), whole(wd[1]), whole(wu[0]), whole(wu[1])]
        + [whole(ub[0]), whole(ub[1]), whole(out_bias), whole(down_bias)]
        + [whole(norm2_gain), whole(norm2_shift)],
        [rows_out(width, BF16)]
        + [rows_out(half, BF16)] * 4
        + [rows_out(width, BF16), rows_out(half, BF16), rows_out(half, BF16)]
        + [rows_out(width, BF16)]
        + [sum_out(1, width)] * 4
        + [sum_out(1, half)] * 2,
        vmem=58 * 2**20,
        mark=0,
    )
    dgain2, dshift2, dbias, ddownb, dupb0, dupb1 = sums2
    step = min(rows, 512)
    got, grads, results, queue, later = {}, {}, {}, [], []
    shapes = {"down": down_weight.shape, "up": up_weight.shape, "out": out_weight.shape}

    def shared(x, side):
        return (
            x,
            pl.BlockSpec(
                (step, x.shape[-1]), lambda i, s: (s[side] * span // step + i, 0)
            ),
        )

    def blocks(x):
        return row_blocks(x, step)

    def trade(**arrays):
        for name, x in arrays.items():
            if isinstance(x, (list, tuple)):
                got[name] = [swap(piece) for piece in line.tie(*x)]
            else:
                (x,) = line.tie(x)
                got[name] = swap(x)

    def begin(chain):
        next(chain)
        queue.append(chain)

    def advance():
        if queue:
            chain = queue.pop(0)
            if next(chain, "end") != "end":
                queue.append(chain)

    def keep_result(name, order):
        def finish(near, far):
            later.append((name, near, far, order))

        return finish

    def do_finish():
        if later:
            name, near, far, order = later.pop(0)
            results[name] = sums.finish(near, far, order, shapes[name])

    def keep_parts(c):
        def finish(near, far):
            grads[c] = (near, far)

        return finish

    def weight(name, order, *operands):
        keep, away = sums.weight_grad(*operands, step, order)
        begin(sums.reduce(keep, away, order, keep_result(name, order)))

    def do_down():
        operands = [blocks(act0), blocks(got["act"]), shared(cotangent, 0), shared(cotangent, 1)]
        weight("down", orders["down"], *operands)

    def do_up():
        weight("up", orders["up"], blocks(h2), blocks(got["h2"]), blocks(dpre0), blocks(got["dpre"]))

    def do_out():
        weight("out", orders["out"], blocks(mixed_o), blocks(mixed_p), blocks(low), blocks(got["low"]))

    each = 2 if items % 2 == 0 else 1
    count = items // each
    wide = each * span

    def do_attend():
        dproj_shape = shaped((3, 2 * rows, half), BF16)
        dmix_own = pl.BlockSpec((wide, half), lambda i, s: (jnp.minimum(i, count - 1), 0))
        dmix_other = pl.BlockSpec((wide, half), lambda i, s: (jnp.maximum(i - count, 0), 0))
        grads["dproj"], *pieces = call(
            partial(
                attend_back_kernel,
                items=items,
                each=each,
                at=[sums.piece_at(order) for order in qkv_orders],
            ),
            scalars,
            (2 * count,),
            [row_blocks(h1, wide), row_blocks(proj, wide), item_blocks(prob, each)]
            + [(dmix0, dmix_own), (got["dmix"], dmix_other)],
            [row_blocks(dproj_shape, wide)] + sums.halves_out(width, half) * 3,
            [pltpu.VMEM((3, width, half), F32)],
            vmem=50 * 2**20,
            mark=0,
        )
        for c in SENDS:
            begin(sums.reduce(pieces[2 * c], pieces[2 * c + 1], qkv_orders[c], keep_parts(c)))

    def do_part():
        grads["part"] = call(
            hidden_grad_kernel,
            scalars,
            grid,
            [row_blocks(grads["dproj"], span, items), whole(qkv)],
            [whole_out((span, width), BF16)] * items,
            vmem=30 * 2**20,
        )

    def do_base():
        dbase, dgain1, dshift1, dtab = call(
            partial(base_grad_kernel, at=lang_at),
            scalars,
            grid,
            [whole(x) for x in got["part"]]
            + [lat, tab, row_blocks(low, span), row_blocks(grads["dproj"], span), whole(qkv), gain1],
            [rows_out(width, F32), sum_out(1, width), sum_out(1, width)]
            + [sum_out(*lang_table.shape)],
            vmem=30 * 2**20,
        )
        results["dbase"] = dbase
        dupb = jnp.where(
            head == 0,
            jnp.concatenate([dupb0, dupb1], axis=1),
            jnp.concatenate([dupb1, dupb0], axis=1),
        )
        small = [dtab, dgain1, dshift1, dbias, dgain2, dshift2, ddownb, dupb]
        begin(
            sum_small(
                line,
                jnp.concatenate(small, axis=0),
                n_dp * n_head,
                lambda x: results.update(small=x),
            )
        )

    def do_qkv():
        results["qkv"] = sums.finish3([grads[c] for c in range(3)], qkv_orders, qkv.shape)

    kernels = {
        "WD": do_down,
        "WU": do_up,
        "WO": do_out,
        "B": do_attend,
        "F": do_finish,
        "H1": do_part,
        "H2": do_base,
        "T1": lambda: trade(act=act1, dmix=dmix1, dpre=dpre1, h2=h2),
        "T2": lambda: trade(low=low),
        "T3": lambda: trade(part=grads["part"]),
    }
    for word in STEPS:
        if word in kernels:
            kernels[word]()
        else:
            for _ in range(word):
                advance()
    while queue:
        advance()
    while later:
        do_finish()
    do_qkv()
    small = results["small"]
    langs = lang_table.shape[0]
    dgain1, dshift1, dbias, dgain2, dshift2, ddownb, dupb = [small[langs + i] for i in range(7)]
    dupb = lax.dynamic_slice_in_dim(dupb, head * half, half, 0)
    return (
        block_out,
        results["dbase"],
        small[:langs],
        dgain1,
        dshift1,
        jnp.transpose(results["qkv"], (1, 0, 2)),
        results["out"],
        dbias,
        dgain2,
        dshift2,
        results["up"],
        dupb,
        results["down"],
        ddownb,
    )


def normalize(values, gain, shift):
    mean = jnp.mean(values, axis=-1, keepdims=True)
    centred = values - mean
    inverse = lax.rsqrt(jnp.mean(centred * centred, axis=-1, keepdims=True) + EPS)
    unit = centred * inverse
    return (unit * gain + shift, unit, inverse)


def normalize_back(grad, unit, inverse, gain):
    scaled = grad * gain
    return inverse * (
        scaled
        - jnp.mean(scaled, axis=-1, keepdims=True)
        - unit * jnp.mean(scaled * unit, axis=-1, keepdims=True)
    )


def own_rows(values, start, share):
    return lax.dynamic_slice_in_dim(values, start, share, 0)


def plain_body(
    latents,
    languages,
    lang_table,
    norm1_gain,
    norm1_shift,
    qkv_weight,
    out_weight,
    out_bias,
    norm2_gain,
    norm2_shift,
    up_weight,
    up_bias,
    down_weight,
    down_bias,
    cotangent,
):
    f32 = jnp.float32
    bf16 = jnp.bfloat16
    items = languages.shape[0]
    rows = latents.shape[0]
    span = rows // items
    width = latents.shape[1]
    local = qkv_weight.shape[2]
    heads_here = local // HEAD_DIM
    scale = HEAD_DIM ** (-0.5)
    share = rows // lax.axis_size("head")
    start = lax.axis_index("head") * share
    token_lang = jnp.repeat(languages, span)
    onehot = (
        token_lang[:, None] == jnp.arange(lang_table.shape[0], dtype=jnp.int32)[None, :]
    ).astype(bf16)
    base = latents.astype(f32) + jnp.dot(onehot, lang_table, preferred_element_type=f32)
    normed1, unit1, inverse1 = normalize(base, norm1_gain, norm1_shift)
    h_one = normed1.astype(bf16)
    qkv_flat = qkv_weight.reshape(width, 3 * local)
    proj = jnp.dot(h_one, qkv_flat, preferred_element_type=f32).astype(bf16)
    proj = proj.reshape(items, span, 3, heads_here, HEAD_DIM)
    query = proj[:, :, 0]
    key = proj[:, :, 1]
    value = proj[:, :, 2]
    raw = jnp.einsum("iqhd,ikhd->ihqk", query, key, preferred_element_type=f32) * scale
    peak = jnp.max(raw, axis=-1, keepdims=True)
    weights = jnp.exp(raw - peak)
    probs = weights / jnp.sum(weights, axis=-1, keepdims=True)
    probs_low = probs.astype(bf16)
    mixed = jnp.einsum("ihqk,ikhd->iqhd", probs_low, value, preferred_element_type=f32)
    mixed = mixed.astype(bf16).reshape(rows, local)
    attn_part = jnp.dot(mixed, out_weight, preferred_element_type=f32)
    attn_full = lax.psum(attn_part, "head")
    middle = base + attn_full + out_bias
    normed2, unit2, inverse2 = normalize(middle, norm2_gain, norm2_shift)
    h_two = normed2.astype(bf16)
    pre = jnp.dot(h_two, up_weight, preferred_element_type=f32) + up_bias
    act, gelu_back = jax.vjp(partial(jax.nn.gelu, approximate=True), pre)
    act_low = act.astype(bf16)
    down_part = jnp.dot(act_low, down_weight, preferred_element_type=f32)
    final = (
        middle + lax.psum(down_part.astype(jnp.bfloat16), "head").astype(jnp.float32) + down_bias
    )
    block_out = own_rows(final, start, share).astype(bf16)
    grad_rows = cotangent.astype(f32)
    d_act = jnp.einsum("td,fd->tf", cotangent, down_weight, preferred_element_type=f32)
    d_down = jnp.einsum("tf,td->fd", act_low, cotangent, preferred_element_type=f32)
    d_pre_low = gelu_back(d_act)[0].astype(bf16)
    d_up = jnp.einsum("td,tf->df", h_two, d_pre_low, preferred_element_type=f32)
    d_up_bias = jnp.sum(d_pre_low.astype(f32), axis=0)
    h2_part = jnp.einsum("tf,df->td", d_pre_low, up_weight, preferred_element_type=f32)
    h2_grad = lax.psum(h2_part, "head")
    d_middle = grad_rows + normalize_back(h2_grad, unit2, inverse2, norm2_gain)
    d_middle_low = d_middle.astype(bf16)
    d_gain2 = jnp.sum(h2_grad * unit2, axis=0)
    d_shift2 = jnp.sum(h2_grad, axis=0)
    d_out_bias = jnp.sum(d_middle, axis=0)
    d_down_bias = jnp.sum(grad_rows, axis=0)
    d_out = jnp.einsum("tc,td->cd", mixed, d_middle_low, preferred_element_type=f32)
    d_mixed = jnp.einsum("td,cd->tc", d_middle_low, out_weight, preferred_element_type=f32)
    d_mixed = d_mixed.astype(bf16).reshape(items, span, heads_here, HEAD_DIM)
    d_probs = jnp.einsum("iqhd,ikhd->ihqk", d_mixed, value, preferred_element_type=f32)
    d_value = jnp.einsum("ihqk,iqhd->ikhd", probs_low, d_mixed, preferred_element_type=f32)
    d_raw = probs * (d_probs - jnp.sum(probs * d_probs, axis=-1, keepdims=True))
    d_raw_low = d_raw.astype(bf16)
    d_query = jnp.einsum("ihqk,ikhd->iqhd", d_raw_low, key, preferred_element_type=f32) * scale
    d_key = jnp.einsum("ihqk,iqhd->ikhd", d_raw_low, query, preferred_element_type=f32) * scale
    d_proj = jnp.stack([d_query, d_key, d_value], axis=2).astype(bf16).reshape(rows, 3 * local)
    d_qkv = jnp.einsum("td,tc->dc", h_one, d_proj, preferred_element_type=f32).reshape(
        width, 3, local
    )
    h1_part = jnp.einsum("tc,dc->td", d_proj, qkv_flat, preferred_element_type=f32)
    h1_grad = lax.psum(h1_part.astype(jnp.bfloat16), "head").astype(jnp.float32)
    d_base = d_middle + normalize_back(h1_grad, unit1, inverse1, norm1_gain)
    onehot_own = onehot.astype(f32)
    input_grad = own_rows(d_base, start, share)
    d_gain1 = jnp.sum(h1_grad * unit1, axis=0)
    d_shift1 = jnp.sum(h1_grad, axis=0)
    d_table = jnp.einsum("tl,td->ld", onehot_own, d_base, precision=HIGH)
    (
        d_qkv,
        d_out,
        d_up,
        d_up_bias,
        d_down,
        d_table,
        d_gain1,
        d_shift1,
        d_out_bias,
        d_gain2,
        d_shift2,
        d_down_bias,
    ) = (
        lax.psum(d_qkv.astype(jnp.bfloat16), "dp").astype(jnp.float32),
        lax.psum(d_out.astype(jnp.bfloat16), "dp").astype(jnp.float32),
        lax.psum(d_up.astype(jnp.bfloat16), "dp").astype(jnp.float32),
        lax.psum(d_up_bias.astype(jnp.bfloat16), "dp").astype(jnp.float32),
        lax.psum(d_down.astype(jnp.bfloat16), "dp").astype(jnp.float32),
        lax.psum(d_table.astype(jnp.bfloat16), "dp").astype(jnp.float32),
        lax.psum(d_gain1.astype(jnp.bfloat16), "dp").astype(jnp.float32),
        lax.psum(d_shift1.astype(jnp.bfloat16), "dp").astype(jnp.float32),
        lax.psum(d_out_bias.astype(jnp.bfloat16), "dp").astype(jnp.float32),
        lax.psum(d_gain2.astype(jnp.bfloat16), "dp").astype(jnp.float32),
        lax.psum(d_shift2.astype(jnp.bfloat16), "dp").astype(jnp.float32),
        lax.psum(d_down_bias.astype(jnp.bfloat16), "dp").astype(jnp.float32),
    )
    return (
        block_out,
        input_grad,
        d_table,
        d_gain1,
        d_shift1,
        d_qkv,
        d_out,
        d_out_bias,
        d_gain2,
        d_shift2,
        d_up,
        d_up_bias,
        d_down,
        d_down_bias,
    )


def solution(mesh):
    in_specs = (
        P("dp", None),
        P("dp"),
        P(),
        P(),
        P(),
        P(None, None, "head"),
        P("head", None),
        P(),
        P(),
        P(),
        P(None, "head"),
        P("head"),
        P("head", None),
        P(),
        P("dp", None),
    )
    out_specs = (
        P(("dp", "head"), None),
        P(("dp", "head"), None),
        P(),
        P(),
        P(),
        P(None, None, "head"),
        P("head", None),
        P(),
        P(),
        P(),
        P(None, "head"),
        P("head"),
        P("head", None),
        P(),
    )
    return jax.shard_map(
        body if mesh.shape["head"] == 2 else plain_body,
         mesh=mesh, in_specs=in_specs, out_specs=out_specs, check_vma=False)
```
